256 devices in a mesh: row: 32 (over y, z), col: 8 (over x, core).
Axes of the slice: x: 4, y: 4, z: 8, core: 2. Of those that a mesh axis runs over, the one named last changes fastest.
Arguments:
- membership: float32 [32768, 512], P(('row', 'col')), may hold values from 0.02 to 0.12
- tile_count: int32 [256], P(('row', 'col')), may hold values from 16 to 128, as said below
- tile_rows: int32 [256, 128], P(('row', 'col')), may hold values from 0 to 7
- tile_cols: int32 [256, 128], P(('row', 'col')), may hold values from 0 to 31
- edge_masks: int32 [256, 128, 128, 128], P(('row', 'col')), may hold values 0 or 1
- neg_rows: int32 [256, 32], P(('row', 'col')), may hold values from 0 to 7
- neg_cols: int32 [256, 32], P(('row', 'col')), may hold values from 0 to 31
- neg_weight: float32 [256, 32], P(('row', 'col')), may hold values from 0.003 to 0.03
Outputs:
- membership_grad: float32 [32768, 512], P(('row', 'col'))
The draws below stay inside these ranges and needn't reach their ends.
Inputs may be any that keep to these rules, and one draw needn't show every extreme that they name: `tile_count`: some device in every draw has all 128 slots live; the others far fewer.
All inputs are finite; a program needn't handle non-finite values. No bound on the sum of `edge_masks` on one device may be relied on, other than what follows from the above.
Results may differ from the reference program's by a relative error of at most 0.0015.
Values may be sent and summed in bfloat16 or wider, within the bound.
No kernel may reach another device: no remote copies, remote signals or barrier semaphores. Data moves between devices by JAX's collectives and lax.ppermute only.
A program may use at most 128 MiB of HBM per device.

```python
import math
import jax
import jax.numpy as jnp
from jax import lax

COMM = 512
TILE_EDGE = 128
NODE_DEV = 128
TILES_DEV = 128
NEG_DEV = 32
ROW_NODES = 1024
COL_NODES = 4096
ROW_TILES = 8
COL_TILES = 32
NODES = 32768
N_ROW = 32
N_COL = 8


def draw_tile_count(key, part):
    key = jax.random.fold_in(key, 11)
    first_key, second_key = jax.random.split(key)
    counts = jax.random.randint(first_key, (N_ROW * N_COL,), TILES_DEV // 8, TILES_DEV // 2 + 1, dtype=jnp.int32)
    chosen = jax.random.randint(second_key, (), 0, N_ROW * N_COL, dtype=jnp.int32)
    return counts.at[chosen].set(TILES_DEV)


def with_ends(array, own_key, smallest, top_value):
    extent = array.shape
    place = [jax.random.randint(jax.random.fold_in(own_key, axis), (), 0, extent[axis]) for axis in range(len(extent))]
    array = array.at[tuple(place)].set(smallest)
    longest = extent.index(max(extent))
    place[longest] = (place[longest] + 1) % extent[longest]
    return array.at[tuple(place)].set(top_value)


def shard_levels(own_key, extent, shards, low, largest):
    loudness, own = 1.0, jax.random.fold_in(own_key, 6)
    for axis_at, blocks in shards:
        draws = jnp.exp(jax.random.uniform(jax.random.fold_in(own, axis_at), (blocks,), jnp.float32, low / len(shards), largest / len(shards)))
        loudness = loudness * jnp.repeat(draws, extent[axis_at] // blocks).reshape([-1 if axis == axis_at else 1 for axis in range(len(extent))])
    return loudness


def setup_inputs(seed: int = 0) -> dict:
    arg_keys = jax.random.split(jax.random.key(seed), 9)
    membership = jnp.clip(jnp.exp(math.log(0.12) - 1.7917595 * jax.random.uniform(arg_keys[0], (NODES, COMM), jnp.float32) ** shard_levels(arg_keys[0], (NODES, COMM), ((0, 256),), -0.2, 0.2)), 0.02, 0.12)
    tile_count = draw_tile_count(jax.random.fold_in(arg_keys[8], 71), 0)
    tile_rows = with_ends(jax.random.randint(arg_keys[2], (N_ROW * N_COL, TILES_DEV), 0, ROW_TILES), jax.random.fold_in(arg_keys[2], 1), 0, ROW_TILES - 1).astype(jnp.int32)
    tile_cols = with_ends(jax.random.randint(arg_keys[3], (N_ROW * N_COL, TILES_DEV), 0, COL_TILES), jax.random.fold_in(arg_keys[3], 1), 0, COL_TILES - 1).astype(jnp.int32)
    edge_masks = with_ends((jax.random.randint(arg_keys[4], (N_ROW * N_COL, TILES_DEV, TILE_EDGE, TILE_EDGE), 0, 8) < 1).astype(jnp.int32), jax.random.fold_in(arg_keys[4], 1), 0, 1)
    neg_rows = with_ends(jax.random.randint(arg_keys[5], (N_ROW * N_COL, NEG_DEV), 0, ROW_TILES), jax.random.fold_in(arg_keys[5], 1), 0, ROW_TILES - 1).astype(jnp.int32)
    neg_cols = with_ends(jax.random.randint(arg_keys[6], (N_ROW * N_COL, NEG_DEV), 0, COL_TILES), jax.random.fold_in(arg_keys[6], 1), 0, COL_TILES - 1).astype(jnp.int32)
    neg_weight = jnp.clip(jnp.exp(math.log(0.03) - 2.3025851 * jax.random.uniform(arg_keys[7], (N_ROW * N_COL, NEG_DEV), jnp.float32) ** shard_levels(arg_keys[7], (N_ROW * N_COL, NEG_DEV), ((0, 256),), -0.2, 0.2)), 0.003, 0.03)
    return dict(membership=membership, tile_count=tile_count, tile_rows=tile_rows, tile_cols=tile_cols, edge_masks=edge_masks, neg_rows=neg_rows, neg_cols=neg_cols, neg_weight=neg_weight)


def device_terms(own_rows, own_cols, rows_list, cols_list, masks, live_count, neg_r, neg_c, neg_w):
    row_blocks = own_rows.reshape(ROW_TILES, TILE_EDGE, COMM)
    col_blocks = own_cols.reshape(COL_TILES, TILE_EDGE, COMM)
    fr_tiles = jnp.take(row_blocks, rows_list, axis=0).astype(jnp.float32)
    fc_tiles = jnp.take(col_blocks, cols_list, axis=0).astype(jnp.float32)
    scores = jnp.einsum('tec,tfc->tef', fr_tiles, fc_tiles)
    live = jnp.arange(TILES_DEV, dtype=jnp.int32) < live_count
    keep = live[:, None, None] & (masks == 1)
    coefficient = jnp.where(keep, -1.0 / jnp.expm1(scores), 0.0).astype(jnp.bfloat16)
    coefficient = lax.optimization_barrier(coefficient).astype(jnp.float32)
    row_tiles_grad = jnp.einsum('tef,tfc->tec', coefficient, fc_tiles)
    col_tiles_grad = jnp.einsum('tef,tec->tfc', coefficient, fr_tiles)
    row_hit = (rows_list[:, None] == jnp.arange(ROW_TILES, dtype=jnp.int32)[None, :]).astype(jnp.float32)
    col_hit = (cols_list[:, None] == jnp.arange(COL_TILES, dtype=jnp.int32)[None, :]).astype(jnp.float32)
    row_grad = jnp.einsum('tk,tec->kec', row_hit, row_tiles_grad)
    col_grad = jnp.einsum('tk,tec->kec', col_hit, col_tiles_grad)
    col_tile_sums = jnp.sum(col_blocks.astype(jnp.float32), axis=1)
    row_tile_sums = jnp.sum(row_blocks.astype(jnp.float32), axis=1)
    neg_row_vec = neg_w[:, None] * jnp.take(col_tile_sums, neg_c, axis=0)
    neg_col_vec = neg_w[:, None] * jnp.take(row_tile_sums, neg_r, axis=0)
    neg_row_hit = (neg_r[:, None] == jnp.arange(ROW_TILES, dtype=jnp.int32)[None, :]).astype(jnp.float32)
    neg_col_hit = (neg_c[:, None] == jnp.arange(COL_TILES, dtype=jnp.int32)[None, :]).astype(jnp.float32)
    row_grad = row_grad + jnp.einsum('nk,nc->kc', neg_row_hit, neg_row_vec)[:, None, :]
    col_grad = col_grad + jnp.einsum('nk,nc->kc', neg_col_hit, neg_col_vec)[:, None, :]
    return row_grad, col_grad


def reference(membership, tile_count, tile_rows, tile_cols, edge_masks, neg_rows, neg_cols, neg_weight):
    panels = membership.astype(jnp.bfloat16).reshape(N_ROW, N_COL, NODE_DEV, COMM)

    def advance(grad_grid, device):
        row_index = device // N_COL
        col_index = device % N_COL
        own_rows = lax.dynamic_index_in_dim(panels, row_index, 0, keepdims=False).reshape(ROW_NODES, COMM)
        own_cols = lax.dynamic_index_in_dim(panels, col_index, 1, keepdims=False).reshape(COL_NODES, COMM)
        row_grad, col_grad = device_terms(own_rows, own_cols, tile_rows[device], tile_cols[device],
                                          edge_masks[device], tile_count[device], neg_rows[device],
                                          neg_cols[device], neg_weight[device])
        grad_grid = grad_grid.at[row_index].add(row_grad.reshape(N_COL, NODE_DEV, COMM))
        grad_grid = grad_grid.at[:, col_index].add(col_grad.reshape(N_ROW, NODE_DEV, COMM))
        return grad_grid, None

    start_grid = jnp.zeros((N_ROW, N_COL, NODE_DEV, COMM), jnp.float32)
    grad_grid, _ = lax.scan(advance, start_grid, jnp.arange(N_ROW * N_COL, dtype=jnp.int32))
    return grad_grid.reshape(NODES, COMM)
```

```python
import functools

import jax
import jax.numpy as jnp
from jax import lax
from jax.experimental import pallas as pl
from jax.experimental.pallas import tpu as pltpu
from jax.sharding import PartitionSpec as P

NY, NZ, NX, NC = 4, 8, 4, 2
T = 128
C = 512
BF = jnp.bfloat16
F32 = jnp.float32
VMEM = pl.BlockSpec(memory_space=pltpu.VMEM)
SMEM = pl.BlockSpec(memory_space=pltpu.SMEM)
PARAMS = pltpu.CompilerParams(vmem_limit_bytes=44 * 1024 * 1024)


def from_y(x, k):
    perm = [(((y + k) % NY) * NZ + z, y * NZ + z) for y in range(NY) for z in range(NZ)]
    return lax.ppermute(x, "row", perm)


def from_z(x, k):
    perm = [(y * NZ + (z + k) % NZ, y * NZ + z) for y in range(NY) for z in range(NZ)]
    return lax.ppermute(x, "row", perm)


def from_x(x, k):
    perm = [(((s + k) % NX) * NC + c, s * NC + c) for s in range(NX) for c in range(NC)]
    return lax.ppermute(x, "col", perm)


def from_core(x):
    perm = [(s * NC + 1 - c, s * NC + c) for s in range(NX) for c in range(NC)]
    return lax.ppermute(x, "col", perm)


def prep_kernel(pos, count, rows, cols, nrows, ncols, nw, masks, m_ref, w_ref):
    y, z, x, c = pos[0], pos[1], pos[2], pos[3]

    def row_at(a):
        return ((a % NC) ^ c) * NX + ((a // NC - x) & (NX - 1))

    def col_at(b):
        return (b % NZ - z) & (NZ - 1), (b // NZ - y) & (NY - 1)

    m_ref[...] = jnp.zeros_like(m_ref)
    for a in range(NX * NC):
        for b in range(NY * NZ):
            w_ref[a, b] = 0.0

    def negative(p, _):
        d, e = col_at(ncols[0, p])
        a = row_at(nrows[0, p])
        w_ref[a, d * NY + e] += nw[0, p]
        return 0

    lax.fori_loop(0, nrows.shape[1], negative, 0)

    def slot(t, _):
        a = row_at(rows[0, t])
        d, e = col_at(cols[0, t])
        at = (d, pl.ds(pl.multiple_of(a * T, T), T), pl.ds(pl.multiple_of(e * T, T), T))
        m_ref[at] += masks[0, t].astype(F32).astype(BF)
        return 0

    lax.fori_loop(0, count[0], slot, 0)


def prep(pos, count, rows, cols, nrows, ncols, nw, masks):
    return pl.pallas_call(
        prep_kernel,
        out_shape=(
            jax.ShapeDtypeStruct((NZ, NX * NC * T, NY * T), BF),
            jax.ShapeDtypeStruct((NX * NC, NY * NZ), F32),
        ),
        in_specs=[SMEM] * 7 + [VMEM],
        out_specs=(VMEM, SMEM),
        compiler_params=PARAMS,
        cost_estimate=pl.CostEstimate(flops=0, bytes_accessed=24 << 20, transcendentals=0),
        name="prep",
    )(pos, count, rows, cols, nrows, ncols, nw, masks)


def dot(a, b, dims):
    return lax.dot_general(a, b, (dims, ((), ())), preferred_element_type=F32)


def chunk_kernel(ds, first, last, w_ref, r_ref, *refs):
    n = len(ds)
    k_refs, refs = refs[:n], refs[n:]
    m_refs, refs = refs[:n], refs[n:]
    if not first:
        acc_in, refs = refs[0], refs[1:]
    if last:
        keep, send, refs = refs[0], refs[1], refs[2:]
        (g_up, g_down, g_acc) = refs
        g_out = None
    else:
        acc_out, refs = refs[0], refs[1:]
        g_out, g_acc = refs[:n], refs[n]
    h = pl.program_id(0)
    half = r_ref[0]
    pick = (
        lax.broadcasted_iota(jnp.int32, (8, 4 * T), 1) // T
        == lax.broadcasted_iota(jnp.int32, (8, 4 * T), 0)
    ).astype(F32).astype(BF)
    row_sums = dot(pick, half, ((1,), (0,)))
    total = None
    neg = [jnp.zeros((1, C), F32) for _ in range(4)]
    for c, d in enumerate(ds):
        k = k_refs[c][...].reshape(NY * T, C)
        s = dot(half, k, ((1,), (1,)))
        coef = (1.0 / (1.0 - jnp.exp(s))).astype(BF)
        coef = coef * m_refs[c][0]
        g = dot(coef, half, ((0,), (0,)))
        r = dot(coef, k, ((1,), (0,)))
        total = r if total is None else total + r
        col_sums = dot(pick, k, ((1,), (0,)))
        for e in range(NY):
            v = jnp.zeros((1, C), F32)
            for f in range(NX):
                w = w_ref[h * NX + f, d * NY + e]
                neg[f] = neg[f] + w * col_sums[e : e + 1]
                v = v + w * row_sums[f : f + 1]
            ge = g[e * T : (e + 1) * T] + v

            @pl.when(h == 0)
            def _():
                g_acc[c, e] = ge

            @pl.when(h == 1)
            def _():
                done = (g_acc[c, e] + ge).astype(BF)
                if g_out is None:
                    if e < 2:
                        g_up[e] = done
                    else:
                        g_down[e - 2] = done
                else:
                    g_out[c][e] = done

    for f in range(NX):
        rows = total[f * T : (f + 1) * T] + neg[f]
        if not first:
            rows = rows + acc_in[0, f * T : (f + 1) * T]
        if last:

            @pl.when(h == 0)
            def _():
                keep[f] = rows

            @pl.when(h == 1)
            def _():
                send[f] = rows
        else:
            acc_out[0, f * T : (f + 1) * T] = rows


def chunk(ds, w, r, ks, m, acc, last=False):
    n = len(ds)
    first = acc is None
    by_half = pl.BlockSpec((1, NX * T, C), lambda h: (h, 0, 0))
    whole = lambda *shape: pl.BlockSpec(shape, lambda h: (0,) * len(shape))
    in_specs = [SMEM, by_half]
    in_specs += [whole(NY, T, C)] * n
    in_specs += [pl.BlockSpec((1, NX * T, NY * T), functools.partial(lambda d, h: (d, h, 0), d)) for d in ds]
    args = [w, r, *ks, *[m] * n]
    if not first:
        in_specs.append(by_half)
        args.append(acc)
    if last:
        shapes = [((NX, T, C), F32)] * 2 + [((2, T, C), BF)] * 2
        out_shape = [jax.ShapeDtypeStruct(*s) for s in shapes]
        out_specs = [whole(*s[0]) for s in shapes]
        aliases = {}
    else:
        out_shape = [jax.ShapeDtypeStruct((2, NX * T, C), F32)]
        out_shape += [jax.ShapeDtypeStruct((NY, T, C), BF)] * n
        out_specs = [by_half] + [whole(NY, T, C)] * n
        aliases = {} if first else {len(args) - 1: 0}
    return pl.pallas_call(
        functools.partial(chunk_kernel, ds, first, last),
        grid=(2,),
        out_shape=out_shape,
        in_specs=in_specs,
        out_specs=out_specs,
        scratch_shapes=[pltpu.VMEM((n, NY, T, C), F32)],
        input_output_aliases=aliases,
        compiler_params=PARAMS,
        cost_estimate=pl.CostEstimate(
            flops=n * 6 * 1024 * 512 * 512, bytes_accessed=(n * 2 + 6) << 20, transcendentals=n * 1024 * 512
        ),
        name="chunk",
    )(*args)


def first_hop_kernel(up, down, up_in, down_in, up_out, down_out):
    up_out[:2] = (up[:2].astype(F32) + up_in[...].astype(F32)).astype(BF)
    up_out[2:] = up[2:]
    down_out[:2] = down[:2]
    down_out[2:] = (down[2:].astype(F32) + down_in[...].astype(F32)).astype(BF)


def hop_kernel(up, down, up_in, down_in, up_out, down_out):
    up_out[...] = (up[...].astype(F32) + up_in[...].astype(F32)).astype(BF)
    down_out[...] = (down[...].astype(F32) + down_in[...].astype(F32)).astype(BF)


def hop(kernel, up, down, up_in, down_in):
    return pl.pallas_call(
        kernel,
        out_shape=[jax.ShapeDtypeStruct(up.shape, BF)] * 2,
        in_specs=[VMEM] * 4,
        out_specs=[VMEM] * 2,
        compiler_params=PARAMS,
        cost_estimate=pl.CostEstimate(flops=1 << 20, bytes_accessed=3 << 20, transcendentals=0),
        name="hop",
    )(up, down, up_in, down_in)


def last_hop_kernel(own, up_in, down_in, keep, *sends):
    for e in range(NY):
        s = own[e].astype(F32) + up_in[e].astype(F32) + down_in[e].astype(F32)
        if e:
            sends[e - 1][...] = s.astype(BF)
        else:
            keep[...] = s


def last_hop(own, up_in, down_in):
    return pl.pallas_call(
        last_hop_kernel,
        out_shape=[jax.ShapeDtypeStruct((T, C), F32)] + [jax.ShapeDtypeStruct((T, C), BF)] * (NY - 1),
        in_specs=[VMEM] * 3,
        out_specs=[VMEM] * NY,
        compiler_params=PARAMS,
        cost_estimate=pl.CostEstimate(flops=1 << 20, bytes_accessed=2 << 20, transcendentals=0),
        name="last_hop",
    )(own, up_in, down_in)


def row_hop_kernel(keep, arrived, own, *sends):
    for f in range(NX):
        s = keep[f] + arrived[f]
        if f:
            sends[f - 1][...] = s
        else:
            own[...] = s


def row_hop(keep, arrived):
    return pl.pallas_call(
        row_hop_kernel,
        out_shape=[jax.ShapeDtypeStruct((T, C), F32)] * NX,
        in_specs=[VMEM] * 2,
        out_specs=[VMEM] * NX,
        compiler_params=PARAMS,
        cost_estimate=pl.CostEstimate(flops=1 << 19, bytes_accessed=3 << 20, transcendentals=0),
        name="row_hop",
    )(keep, arrived)


def final_kernel(*refs):
    out = refs[-1]
    s = refs[0][...]
    for r in refs[1:-1]:
        s = s + r[...].astype(F32)
    out[...] = s


def final(*terms):
    return pl.pallas_call(
        final_kernel,
        out_shape=jax.ShapeDtypeStruct((T, C), F32),
        in_specs=[VMEM] * len(terms),
        out_specs=VMEM,
        compiler_params=PARAMS,
        name="final",
    )(*terms)


def local(membership, tile_count, tile_rows, tile_cols, edge_masks, neg_rows, neg_cols, neg_weight):
    i, j = lax.axis_index("row"), lax.axis_index("col")
    pos = jnp.stack([i // NZ, i % NZ, j // NC, j % NC]).astype(jnp.int32)
    shard = membership.astype(BF)
    block = jnp.stack([shard] + [from_y(shard, k) for k in (1, 2, 3)])
    same = jnp.stack([shard] + [from_x(shard, k) for k in (1, 2, 3)])
    r = jnp.stack([same, from_core(same)]).reshape(2, NX * T, C)
    m, w = prep(pos, tile_count, tile_rows, tile_cols, neg_rows, neg_cols, neg_weight, edge_masks)

    above = [block]
    below = [block]
    for _ in range(3):
        above.append(from_z(above[-1], 1))
        below.append(from_z(below[-1], -1))
    far = jnp.concatenate([from_z(above[3][:2], 1), from_z(below[3][2:], -1)])

    acc, g0 = chunk((0,), w, r, [block], m, None)
    acc, g1, g7 = chunk((1, 7), w, r, [above[1], below[1]], m, acc)
    acc, g2, g6 = chunk((2, 6), w, r, [above[2], below[2]], m, acc)
    acc, g3, g5 = chunk((3, 5), w, r, [above[3], below[3]], m, acc)
    row_keep, row_send, g_up, g_down = chunk((4,), w, r, [far], m, acc, last=True)

    up, down = g_up, g_down
    up, down = hop(first_hop_kernel, g3, g5, from_z(up, -1), from_z(down, 1))
    up, down = hop(hop_kernel, g2, g6, from_z(up, -1), from_z(down, 1))
    up, down = hop(hop_kernel, g1, g7, from_z(up, -1), from_z(down, 1))
    own, s1, s2, s3 = last_hop(g0, from_z(up, -1), from_z(down, 1))
    col_parts = [own, from_y(s1, -1), from_y(s2, -2), from_y(s3, -3)]

    row_own, r1, r2, r3 = row_hop(row_keep, from_core(row_send))
    row_parts = [row_own, from_x(r1, -1), from_x(r2, -2), from_x(r3, -3)]
    return final(*row_parts, *col_parts)


def solution(mesh):
    placed = (
        P(("row", "col"), None),
        P(("row", "col")),
        P(("row", "col"), None),
        P(("row", "col"), None),
        P(("row", "col"), None, None, None),
        P(("row", "col"), None),
        P(("row", "col"), None),
        P(("row", "col"), None),
    )
    return jax.shard_map(
        local, mesh=mesh, in_specs=placed, out_specs=P(("row", "col"), None), check_vma=False
    )
```

```python
import functools

import jax
import jax.numpy as jnp
from jax import lax
from jax.experimental import pallas as pl
from jax.experimental.pallas import tpu as pltpu
from jax.sharding import PartitionSpec as P

NY, NZ, NX, NC = 4, 8, 4, 2
T = 128
C = 512
BF = jnp.bfloat16
F32 = jnp.float32
VMEM = pl.BlockSpec(memory_space=pltpu.VMEM)
SMEM = pl.BlockSpec(memory_space=pltpu.SMEM)
PARAMS = pltpu.CompilerParams(vmem_limit_bytes=28 * 1024 * 1024)
SLOTS = 16
BUFFERS = 4
PIECES = ((0, 256), (256, 512))


def from_y(x, k):
    perm = [(((y + k) % NY) * NZ + z, y * NZ + z) for y in range(NY) for z in range(NZ)]
    return lax.ppermute(x, "row", perm)


def from_z(x, k):
    perm = [(y * NZ + (z + k) % NZ, y * NZ + z) for y in range(NY) for z in range(NZ)]
    return lax.ppermute(x, "row", perm)


def from_x(x, k):
    perm = [(((s + k) % NX) * NC + c, s * NC + c) for s in range(NX) for c in range(NC)]
    return lax.ppermute(x, "col", perm)


def from_core(x):
    perm = [(s * NC + 1 - c, s * NC + c) for s in range(NX) for c in range(NC)]
    return lax.ppermute(x, "col", perm)


def prep_kernel(ints, nw, masks, m_ref, w_ref, buf, sem):
    n_slots, n_neg = masks.shape[1], nw.shape[1]
    at_neg, at_pos = 2 * n_slots, 2 * (n_slots + n_neg)
    count = ints[at_pos + 4]
    y, z, x, c = ints[at_pos], ints[at_pos + 1], ints[at_pos + 2], ints[at_pos + 3]
    n_blocks = masks.shape[1] // SLOTS

    def fetch(b):
        at = b % BUFFERS
        return pltpu.make_async_copy(masks.at[0, pl.ds(b * SLOTS, SLOTS)], buf.at[at], sem.at[at])

    for b in range(BUFFERS):
        fetch(b).start()

    def row_at(a):
        return ((a % NC) ^ c) * NX + ((a // NC - x) & (NX - 1))

    def col_at(b):
        return (b % NZ - z) & (NZ - 1), (b // NZ - y) & (NY - 1)

    m_ref[...] = jnp.zeros_like(m_ref)
    for a in range(NX * NC):
        for b in range(NY * NZ):
            w_ref[a, b] = 0.0

    def negative(p, _):
        d, e = col_at(ints[at_neg + n_neg + p])
        a = row_at(ints[at_neg + p])
        w_ref[a, d * NY + e] += nw[0, p]
        return 0

    lax.fori_loop(0, n_neg, negative, 0)

    for b in range(n_blocks):
        fetch(b).wait()

        def slot(t, _):
            a = row_at(ints[b * SLOTS + t])
            d, e = col_at(ints[n_slots + b * SLOTS + t])
            at = (d, pl.ds(pl.multiple_of(a * T, T), T), pl.ds(pl.multiple_of(e * T, T), T))
            m_ref[at] += buf[b % BUFFERS, t].astype(F32).astype(BF)
            return 0

        lax.fori_loop(0, jnp.clip(count - b * SLOTS, 0, SLOTS), slot, 0)
        if b + BUFFERS < n_blocks:
            fetch(b + BUFFERS).start()


def prep(ints, nw, masks):
    return pl.pallas_call(
        prep_kernel,
        out_shape=(
            jax.ShapeDtypeStruct((NZ, NX * NC * T, NY * T), BF),
            jax.ShapeDtypeStruct((NX * NC, NY * NZ), F32),
        ),
        in_specs=[SMEM, SMEM, pl.BlockSpec(memory_space=pltpu.HBM)],
        out_specs=(VMEM, SMEM),
        scratch_shapes=[pltpu.VMEM((BUFFERS, SLOTS, T, T), jnp.int32), pltpu.SemaphoreType.DMA((BUFFERS,))],
        compiler_params=pltpu.CompilerParams(vmem_limit_bytes=45 * 1024 * 1024),
        cost_estimate=pl.CostEstimate(flops=0, bytes_accessed=16 << 20, transcendentals=0),
        name="prep",
    )(ints, nw, masks)


def dot(a, b, dims):
    return lax.dot_general(a, b, (dims, ((), ())), preferred_element_type=F32)


def tile_sums(x):
    return [jnp.sum(x[e * T : (e + 1) * T].astype(F32), axis=0, keepdims=True) for e in range(x.shape[0] // T)]


def chunk_kernel(ds, first, last, split, w_ref, r_ref, *refs):
    n, p = len(ds), len(PIECES)
    k_refs, refs = refs[:n], refs[n:]
    m_refs, refs = refs[:n], refs[n:]
    if not first:
        acc_in, refs = refs[0], refs[1:]
    halves = [r_ref[0], r_ref[1]]
    row_sums = tile_sums(halves[0]) + tile_sums(halves[1])
    neg = [jnp.zeros((1, C), F32) for _ in range(NX * NC)]
    total = [None, None]
    grads = []
    for c, d in enumerate(ds):
        k = k_refs[c][...].reshape(NY * T, C)
        col_sums = tile_sums(k)
        grad = None
        for h in range(2):
            s = dot(halves[h], k, ((1,), (1,)))
            coef = (1.0 / (1.0 - jnp.exp(s))).astype(BF) * m_refs[c][0, h * NX * T : (h + 1) * NX * T]
            g = dot(coef, halves[h], ((0,), (0,)))
            r = dot(coef, k, ((1,), (0,)))
            grad = g if grad is None else grad + g
            total[h] = r if total[h] is None else total[h] + r
        tiles = []
        for e in range(NY):
            v = jnp.zeros((1, C), F32)
            for a in range(NX * NC):
                weight = w_ref[a, d * NY + e]
                neg[a] = neg[a] + weight * col_sums[e]
                v = v + weight * row_sums[a]
            tiles.append((grad[e * T : (e + 1) * T] + v).astype(BF))
        grads.append(tiles)
    for a in range(NX * NC):
        h, f = a // NX, a % NX
        rows = total[h][f * T : (f + 1) * T] + neg[a]
        if not first:
            rows = rows + acc_in[h, f * T : (f + 1) * T]
        if last:
            refs[h][f] = rows
        else:
            refs[0][h, f * T : (f + 1) * T] = rows
    refs = refs[2 if last else 1 :]
    for c in range(n):
        for e in range(NY):
            if split:
                refs[e // 2][e % 2] = grads[c][e]
                continue
            for q, (lo, hi) in enumerate(PIECES):
                refs[c * p + q][e] = grads[c][e][:, lo:hi]


def chunk(ds, w, r, ks, m, acc, last=False, split=False):
    n, p = len(ds), len(PIECES)
    first = acc is None
    whole = lambda *shape: pl.BlockSpec(shape, lambda h: (0,) * len(shape))
    in_specs = [SMEM, whole(2, NX * T, C)] + [whole(NY, T, C)] * n
    in_specs += [pl.BlockSpec((1, NX * NC * T, NY * T), functools.partial(lambda d, h: (d, 0, 0), d)) for d in ds]
    args = [w, r, *ks, *[m] * n]
    if not first:
        in_specs.append(whole(2, NX * T, C))
        args.append(acc)
    shapes = [((NX, T, C), F32)] * 2 if last else [((2, NX * T, C), F32)]
    if split:
        shapes += [((2, T, C), BF)] * 2
    else:
        shapes += [((NY, T, hi - lo), BF) for _ in ds for lo, hi in PIECES]
    out = pl.pallas_call(
        functools.partial(chunk_kernel, ds, first, last, split),
        grid=(1,),
        out_shape=[jax.ShapeDtypeStruct(*s) for s in shapes],
        in_specs=in_specs,
        out_specs=[whole(*s[0]) for s in shapes],
        input_output_aliases={} if first or last else {len(args) - 1: 0},
        compiler_params=PARAMS,
        cost_estimate=pl.CostEstimate(
            flops=n * 6 * 1024 * 512 * 512, bytes_accessed=(n * 2 + 6) << 20, transcendentals=n * 1024 * 512
        ),
        name="chunk",
    )(*args)
    rows, out = (out[:2], out[2:]) if last else (out[:1], out[1:])
    if split:
        return *rows, out
    return *rows, *[out[c * p : (c + 1) * p] for c in range(n)]


def first_hop_kernel(up_in, down_in, *refs):
    p = len(PIECES)
    ups, downs, up_outs, down_outs = refs[:p], refs[p : 2 * p], refs[2 * p : 3 * p], refs[3 * p :]
    for q, (lo, hi) in enumerate(PIECES):
        up_outs[q][:2] = (ups[q][:2].astype(F32) + up_in[:, :, lo:hi].astype(F32)).astype(BF)
        up_outs[q][2:] = ups[q][2:]
        down_outs[q][:2] = downs[q][:2]
        down_outs[q][2:] = (downs[q][2:].astype(F32) + down_in[:, :, lo:hi].astype(F32)).astype(BF)


def first_hop(up_in, down_in, ups, downs):
    own = [*ups, *downs]
    out = pl.pallas_call(
        first_hop_kernel,
        out_shape=[jax.ShapeDtypeStruct(x.shape, BF) for x in own],
        in_specs=[VMEM] * (2 + len(own)),
        out_specs=[VMEM] * len(own),
        compiler_params=PARAMS,
        cost_estimate=pl.CostEstimate(flops=1 << 20, bytes_accessed=3 << 20, transcendentals=0),
        name="first_hop",
    )(up_in, down_in, *own)
    return list(out[: len(ups)]), list(out[len(ups) :])


def hop_kernel(up, down, up_in, down_in, up_out, down_out):
    up_out[...] = (up[...].astype(F32) + up_in[...].astype(F32)).astype(BF)
    down_out[...] = (down[...].astype(F32) + down_in[...].astype(F32)).astype(BF)


def hop(kernel, up, down, up_in, down_in):
    return pl.pallas_call(
        kernel,
        out_shape=[jax.ShapeDtypeStruct(up.shape, BF)] * 2,
        in_specs=[VMEM] * 4,
        out_specs=[VMEM] * 2,
        compiler_params=PARAMS,
        cost_estimate=pl.CostEstimate(flops=1 << 20, bytes_accessed=3 << 20, transcendentals=0),
        name="hop",
    )(up, down, up_in, down_in)


def last_hop_kernel(own, up_in, down_in, keep, *sends):
    for e in range(NY):
        s = own[e].astype(F32) + up_in[e].astype(F32) + down_in[e].astype(F32)
        if e:
            sends[e - 1][...] = s.astype(BF)
        else:
            keep[...] = s


def last_hop(own, up_in, down_in):
    return pl.pallas_call(
        last_hop_kernel,
        out_shape=[jax.ShapeDtypeStruct(own.shape[1:], F32)] + [jax.ShapeDtypeStruct(own.shape[1:], BF)] * (NY - 1),
        in_specs=[VMEM] * 3,
        out_specs=[VMEM] * NY,
        compiler_params=PARAMS,
        cost_estimate=pl.CostEstimate(flops=1 << 20, bytes_accessed=2 << 20, transcendentals=0),
        name="last_hop",
    )(own, up_in, down_in)


def row_hop_kernel(keep, arrived, own, *sends):
    for f in range(NX):
        s = keep[f] + arrived[f]
        if f:
            sends[f - 1][...] = s.astype(BF)
        else:
            own[...] = s


def row_hop(keep, arrived):
    return pl.pallas_call(
        row_hop_kernel,
        out_shape=[jax.ShapeDtypeStruct((T, C), F32)] + [jax.ShapeDtypeStruct((T, C), BF)] * (NX - 1),
        in_specs=[VMEM] * 2,
        out_specs=[VMEM] * NX,
        compiler_params=PARAMS,
        cost_estimate=pl.CostEstimate(flops=1 << 19, bytes_accessed=3 << 20, transcendentals=0),
        name="row_hop",
    )(keep, arrived)


def final_kernel(*refs):
    out = refs[-1]
    rows = refs[0][...]
    for part in refs[1:NX]:
        rows = rows + part[...].astype(F32)
    for q, (lo, hi) in enumerate(PIECES):
        own, *sent = refs[NX + q * NY : NX + (q + 1) * NY]
        cols = own[...]
        for part in sent:
            cols = cols + part[...].astype(F32)
        out[:, lo:hi] = rows[:, lo:hi] + cols


def final(*terms):
    return pl.pallas_call(
        final_kernel,
        out_shape=jax.ShapeDtypeStruct((T, C), F32),
        in_specs=[VMEM] * len(terms),
        out_specs=VMEM,
        compiler_params=PARAMS,
        name="final",
    )(*terms)


def tie(x, *tokens):
    return lax.optimization_barrier((x, *tokens))[0]


def local(membership, tile_count, tile_rows, tile_cols, edge_masks, neg_rows, neg_cols, neg_weight):
    i, j = lax.axis_index("row"), lax.axis_index("col")
    pos = jnp.stack([i // NZ, i % NZ, j // NC, j % NC]).astype(jnp.int32)
    ints = jnp.concatenate([tile_rows[0], tile_cols[0], neg_rows[0], neg_cols[0], pos, tile_count])
    shard = membership.astype(BF)
    stack = [shard] + [from_y(shard, k) for k in (1, 2, 3)]
    first = jnp.stack(stack)
    same = jnp.stack([shard] + [from_x(shard, k) for k in (1, 2, 3)])
    m, w = prep(tie(ints, first), neg_weight, edge_masks)
    p = range(len(PIECES))

    above, below = [first], [first]

    def step(*token):
        up, down = tie((above[-1], below[-1]), *token)
        above.append(from_z(up, 1))
        below.append(from_z(down, -1))

    step()
    r = jnp.stack([same, from_core(tie(same, m))]).reshape(2, NX * T, C)
    step(m)
    acc, g0 = chunk((0,), tie(w, above[1]), r, [first], m, None)
    acc, g1, g7 = chunk((1, 7), w, r, [above[1], below[1]], m, acc)
    step(acc)
    acc, g2, g6 = chunk((2, 6), w, r, [above[2], below[2]], m, acc)
    up, down = tie((above[3], below[3]), acc)
    far_up, far_down = from_z(up[:2], 1), from_z(down[2:], -1)
    acc, g3, g5 = chunk((3, 5), w, r, [above[3], below[3]], m, acc)
    far = jnp.concatenate([tie(far_up, acc), far_down])
    row_keep, row_send, g4 = chunk((4,), w, r, [far], m, acc, last=True, split=True)

    def arrive(up, down):
        return [from_z(up[q], -1) for q in p], [from_z(down[q], 1) for q in p]

    def hops(kernel, up_in, down_in, up_own, down_own):
        pairs = [hop(kernel, up_own[q], down_own[q], up_in[q], down_in[q]) for q in p]
        return [x[0] for x in pairs], [x[1] for x in pairs]

    up_in, down_in = from_z(g4[0], -1), from_z(g4[1], 1)
    row_own, *row_sends = row_hop(row_keep, from_core(row_send))
    up, down = first_hop(*tie((up_in, down_in), row_own), g3, g5)
    up_in, down_in = arrive(up, down)
    row_parts = [row_own] + [from_x(row_sends[k - 1], -k) for k in (1, 2, 3)]
    up_in[1], down_in[1] = tie((up_in[1], down_in[1]), *row_parts)
    up, down = hops(hop_kernel, up_in, down_in, g2, g6)
    up, down = hops(hop_kernel, *arrive(up, down), g1, g7)
    up_in, down_in = arrive(up, down)
    col_parts = []
    for q in p:
        own, s1, s2, s3 = last_hop(g0[q], up_in[q], down_in[q])
        col_parts += [own, from_y(s1, -1), from_y(s2, -2), from_y(s3, -3)]
    return final(*row_parts, *col_parts)


def solution(mesh):
    placed = (
        P(("row", "col"), None),
        P(("row", "col")),
        P(("row", "col"), None),
        P(("row", "col"), None),
        P(("row", "col"), None, None, None),
        P(("row", "col"), None),
        P(("row", "col"), None),
        P(("row", "col"), None),
    )
    return jax.shard_map(
        local, mesh=mesh, in_specs=placed, out_specs=P(("row", "col"), None), check_vma=False
    )
```

```python
import functools

import jax
import jax.numpy as jnp
from jax import lax
from jax.experimental import pallas as pl
from jax.experimental.pallas import tpu as pltpu
from jax.sharding import PartitionSpec as P

NY, NZ, NX, NC = 4, 8, 4, 2
T = 128
C = 512
BF = jnp.bfloat16
F32 = jnp.float32
VMEM = pl.BlockSpec(memory_space=pltpu.VMEM)
SMEM = pl.BlockSpec(memory_space=pltpu.SMEM)
PARAMS = pltpu.CompilerParams(vmem_limit_bytes=28 * 1024 * 1024)
SLOTS = 16
BUFFERS = 4
PIECES = ((0, 256), (256, 512))


def from_y(x, k):
    perm = [(((y + k) % NY) * NZ + z, y * NZ + z) for y in range(NY) for z in range(NZ)]
    return lax.ppermute(x, "row", perm)


def from_z(x, k):
    perm = [(y * NZ + (z + k) % NZ, y * NZ + z) for y in range(NY) for z in range(NZ)]
    return lax.ppermute(x, "row", perm)


def from_x(x, k):
    perm = [(((s + k) % NX) * NC + c, s * NC + c) for s in range(NX) for c in range(NC)]
    return lax.ppermute(x, "col", perm)


def from_core(x):
    perm = [(s * NC + 1 - c, s * NC + c) for s in range(NX) for c in range(NC)]
    return lax.ppermute(x, "col", perm)


def prep_kernel(ints, nw, masks, m_ref, w_ref, buf, sem):
    n_slots, n_neg = masks.shape[1], nw.shape[1]
    at_neg, at_pos = 2 * n_slots, 2 * (n_slots + n_neg)
    count = ints[at_pos + 4]
    y, z, x, c = ints[at_pos], ints[at_pos + 1], ints[at_pos + 2], ints[at_pos + 3]
    n_blocks = masks.shape[1] // SLOTS

    def fetch(b):
        at = b % BUFFERS
        return pltpu.make_async_copy(masks.at[0, pl.ds(b * SLOTS, SLOTS)], buf.at[at], sem.at[at])

    for b in range(BUFFERS):
        fetch(b).start()

    def row_at(a):
        return ((a % NC) ^ c) * NX + ((a // NC - x) & (NX - 1))

    def col_at(b):
        return (b % NZ - z) & (NZ - 1), (b // NZ - y) & (NY - 1)

    m_ref[...] = jnp.zeros_like(m_ref)

    for a in range(NX * NC):
        for b in range(NY * NZ):
            w_ref[a, b] = 0.0

    def negative(p, _):
        d, e = col_at(ints[at_neg + n_neg + p])
        a = row_at(ints[at_neg + p])
        w_ref[a, d * NY + e] += nw[0, p]
        return 0

    lax.fori_loop(0, n_neg, negative, 0)

    def block(b, _):
        fetch(b).wait()

        def slot(t, _):
            a = row_at(ints[b * SLOTS + t])
            d, e = col_at(ints[n_slots + b * SLOTS + t])
            at = (d, pl.ds(pl.multiple_of(a * T, T), T), pl.ds(pl.multiple_of(e * T, T), T))
            m_ref[at] += buf[b % BUFFERS, t].astype(F32).astype(BF)
            return 0

        lax.fori_loop(0, jnp.clip(count - b * SLOTS, 0, SLOTS), slot, 0)

        @pl.when(b + BUFFERS < n_blocks)
        def _():
            fetch(b + BUFFERS).start()

        return 0

    lax.fori_loop(0, n_blocks, block, 0)


def prep(ints, nw, masks):
    return pl.pallas_call(
        prep_kernel,
        out_shape=(
            jax.ShapeDtypeStruct((NZ, NX * NC * T, NY * T), BF),
            jax.ShapeDtypeStruct((NX * NC, NY * NZ), F32),
        ),
        in_specs=[SMEM, SMEM, pl.BlockSpec(memory_space=pltpu.HBM)],
        out_specs=(VMEM, SMEM),
        scratch_shapes=[pltpu.VMEM((BUFFERS, SLOTS, T, T), jnp.int32), pltpu.SemaphoreType.DMA((BUFFERS,))],
        compiler_params=pltpu.CompilerParams(vmem_limit_bytes=45 * 1024 * 1024),
        cost_estimate=pl.CostEstimate(flops=0, bytes_accessed=16 << 20, transcendentals=0),
        name="prep",
    )(ints, nw, masks)


def dot(a, b, dims):
    return lax.dot_general(a, b, (dims, ((), ())), preferred_element_type=F32)


def row_sums_kernel(r_ref, out):
    def body(h, _):
        for f in range(NX):
            out[h, f : f + 1] = jnp.sum(r_ref[h, f * T : (f + 1) * T].astype(F32), axis=0, keepdims=True)
        return 0

    lax.fori_loop(0, 2, body, 0)


def row_sums(r):
    return pl.pallas_call(
        row_sums_kernel,
        out_shape=jax.ShapeDtypeStruct((2, 8, C), F32),
        in_specs=[VMEM],
        out_specs=VMEM,
        compiler_params=PARAMS,
        name="row_sums",
    )(r)


def chunk_kernel(ds, first, split, w_ref, r_ref, row_sums, *refs):
    n = len(ds)
    k_refs, refs = refs[:n], refs[n:]
    m_ref, refs = refs[0], refs[1:]
    if not first:
        acc_in, refs = refs[0], refs[1:]
    p = len(PIECES)
    rows_out, refs, (g_acc, k_all, col_sums) = refs[0], refs[1:-3], refs[-3:]
    for c in range(n):
        for e in range(NY):
            g_acc[c, e * T : (e + 1) * T] = jnp.zeros((T, C), F32)
            k_all[c, e * T : (e + 1) * T] = k_refs[c][e]
            col_sums[c, e : e + 1] = jnp.sum(k_refs[c][e].astype(F32), axis=0, keepdims=True)

    def body(step, _):
        c, h = step // 2, step % 2
        d = ds[0] if n == 1 else jnp.where(c == 0, ds[0], ds[1])
        x, k = r_ref[h], k_all[c]
        s = dot(x, k, ((1,), (1,)))
        at = pl.ds(pl.multiple_of(h * NX * T, NX * T), NX * T)
        coef = (1.0 / (1.0 - jnp.exp(s))).astype(BF) * m_ref[d, at]
        g = dot(coef, x, ((0,), (0,)))
        r = dot(coef, k, ((1,), (0,)))
        sums = [row_sums[h, f : f + 1] for f in range(NX)]
        weights = [[w_ref[h * NX + f, d * NY + e] for e in range(NY)] for f in range(NX)]
        for e in range(NY):
            v = sum(weights[f][e] * sums[f] for f in range(NX))
            g_acc[c, e * T : (e + 1) * T] += g[e * T : (e + 1) * T] + v
        for f in range(NX):
            v = sum(weights[f][e] * col_sums[c, e : e + 1] for e in range(NY))
            rows = r[f * T : (f + 1) * T] + v
            base = 0.0 if first and n == 1 else (rows_out if first else acc_in)[h, f * T : (f + 1) * T]
            rows_out[h, f * T : (f + 1) * T] = rows + base
        return 0

    lax.fori_loop(0, 2 * n, body, 0)
    for c in range(n):
        for e in range(NY):
            done = g_acc[c, e * T : (e + 1) * T].astype(BF)
            if split:
                refs[e // 2][e % 2] = done
                continue
            for q, (lo, hi) in enumerate(PIECES):
                refs[c * p + q][e] = done[:, lo:hi]


def chunk(ds, w, rows, ks, m, acc, split=False):
    n, p = len(ds), len(PIECES)
    first = acc is None
    args = [w, *rows, *ks, m] + ([] if first else [acc])
    shapes = [((2, NX * T, C), F32)]
    if split:
        shapes += [((2, T, C), BF)] * 2
    else:
        shapes += [((NY, T, hi - lo), BF) for _ in ds for lo, hi in PIECES]
    out = pl.pallas_call(
        functools.partial(chunk_kernel, ds, first, split),
        out_shape=[jax.ShapeDtypeStruct(*s) for s in shapes],
        in_specs=[SMEM] + [VMEM] * (len(args) - 1),
        out_specs=[VMEM] * len(shapes),
        scratch_shapes=[pltpu.VMEM((n, NY * T, C), F32), pltpu.VMEM((n, NY * T, C), BF), pltpu.VMEM((n, 8, C), F32)],
        input_output_aliases={} if first else {len(args) - 1: 0},
        compiler_params=PARAMS,
        cost_estimate=pl.CostEstimate(
            flops=n * 6 * 1024 * 512 * 512, bytes_accessed=(n * 2 + 6) << 20, transcendentals=n * 1024 * 512
        ),
        name="chunk",
    )(*args)
    if split:
        return out
    return out[0], *[out[1 + c * p : 1 + (c + 1) * p] for c in range(n)]


def first_hop_kernel(up_in, down_in, *refs):
    p = len(PIECES)
    ups, downs, up_outs, down_outs = refs[:p], refs[p : 2 * p], refs[2 * p : 3 * p], refs[3 * p :]
    for q, (lo, hi) in enumerate(PIECES):
        up_outs[q][:2] = (ups[q][:2].astype(F32) + up_in[:, :, lo:hi].astype(F32)).astype(BF)
        up_outs[q][2:] = ups[q][2:]
        down_outs[q][:2] = downs[q][:2]
        down_outs[q][2:] = (downs[q][2:].astype(F32) + down_in[:, :, lo:hi].astype(F32)).astype(BF)


def first_hop(up_in, down_in, ups, downs):
    own = [*ups, *downs]
    out = pl.pallas_call(
        first_hop_kernel,
        out_shape=[jax.ShapeDtypeStruct(x.shape, BF) for x in own],
        in_specs=[VMEM] * (2 + len(own)),
        out_specs=[VMEM] * len(own),
        compiler_params=PARAMS,
        cost_estimate=pl.CostEstimate(flops=1 << 20, bytes_accessed=3 << 20, transcendentals=0),
        name="first_hop",
    )(up_in, down_in, *own)
    return list(out[: len(ups)]), list(out[len(ups) :])


def hop_kernel(up, down, up_in, down_in, up_out, down_out):
    up_out[...] = (up[...].astype(F32) + up_in[...].astype(F32)).astype(BF)
    down_out[...] = (down[...].astype(F32) + down_in[...].astype(F32)).astype(BF)


def hop(kernel, up, down, up_in, down_in):
    return pl.pallas_call(
        kernel,
        out_shape=[jax.ShapeDtypeStruct(up.shape, BF)] * 2,
        in_specs=[VMEM] * 4,
        out_specs=[VMEM] * 2,
        compiler_params=PARAMS,
        cost_estimate=pl.CostEstimate(flops=1 << 20, bytes_accessed=3 << 20, transcendentals=0),
        name="hop",
    )(up, down, up_in, down_in)


def last_hop_kernel(*refs):
    p = len(PIECES)
    keep, *sends = refs[3 * p :]
    for q, (lo, hi) in enumerate(PIECES):
        for e in range(NY):
            s = sum(refs[k * p + q][e].astype(F32) for k in range(3))
            if e:
                sends[e - 1][:, lo:hi] = s.astype(BF)
            else:
                keep[:, lo:hi] = s


def last_hop(own, up_in, down_in):
    args = [*own, *up_in, *down_in]
    return pl.pallas_call(
        last_hop_kernel,
        out_shape=[jax.ShapeDtypeStruct((T, C), F32)] + [jax.ShapeDtypeStruct((T, C), BF)] * (NY - 1),
        in_specs=[VMEM] * len(args),
        out_specs=[VMEM] * NY,
        compiler_params=PARAMS,
        cost_estimate=pl.CostEstimate(flops=1 << 20, bytes_accessed=2 << 20, transcendentals=0),
        name="last_hop",
    )(*args)


def row_hop_kernel(keep, arrived, own, *sends):
    for f in range(NX):
        s = keep[0, f * T : (f + 1) * T] + arrived[f * T : (f + 1) * T]
        if f:
            sends[f - 1][...] = s.astype(BF)
        else:
            own[...] = s


def row_hop(keep, arrived):
    return pl.pallas_call(
        row_hop_kernel,
        out_shape=[jax.ShapeDtypeStruct((T, C), F32)] + [jax.ShapeDtypeStruct((T, C), BF)] * (NX - 1),
        in_specs=[VMEM] * 2,
        out_specs=[VMEM] * NX,
        compiler_params=PARAMS,
        cost_estimate=pl.CostEstimate(flops=1 << 19, bytes_accessed=3 << 20, transcendentals=0),
        name="row_hop",
    )(keep, arrived)


def final_kernel(*refs):
    out = refs[-1]
    total = refs[0][...]
    for part in refs[1:-1]:
        total = total + part[...].astype(F32)
    out[...] = total


def final(*terms):
    return pl.pallas_call(
        final_kernel,
        out_shape=jax.ShapeDtypeStruct((T, C), F32),
        in_specs=[VMEM] * len(terms),
        out_specs=VMEM,
        compiler_params=PARAMS,
        name="final",
    )(*terms)


def tie(x, *tokens):
    return lax.optimization_barrier((x, *tokens))[0]


def local(membership, tile_count, tile_rows, tile_cols, edge_masks, neg_rows, neg_cols, neg_weight):
    i, j = lax.axis_index("row"), lax.axis_index("col")
    pos = jnp.stack([i // NZ, i % NZ, j // NC, j % NC]).astype(jnp.int32)
    ints = jnp.concatenate([tile_rows[0], tile_cols[0], neg_rows[0], neg_cols[0], pos, tile_count])
    shard = membership.astype(BF)
    next_y, last_y = from_y(shard, 1), from_y(shard, -1)
    half = T // 2
    far_y = jnp.concatenate([from_y(next_y[:half], 1), from_y(last_y[half:], -1)])
    stack = [shard, next_y, far_y, last_y]
    first = jnp.stack(stack)
    same = jnp.stack([shard] + [from_x(shard, k) for k in (1, 2, 3)])
    m, w = prep(tie(ints, first), neg_weight, edge_masks)
    p = range(len(PIECES))

    above, below = [first], [first]

    def step(*token):
        up, down = tie((above[-1], below[-1]), *token)
        above.append(from_z(up, 1))
        below.append(from_z(down, -1))

    step()
    r = jnp.stack([same, from_core(tie(same, m))]).reshape(2, NX * T, C)
    rows = r, row_sums(r)
    step(m)
    acc, g0 = chunk((0,), tie(w, above[1]), rows, [first], m, None)
    acc, g1, g7 = chunk((1, 7), w, rows, [above[1], below[1]], m, acc)
    step(acc)
    acc, g2, g6 = chunk((2, 6), w, rows, [above[2], below[2]], m, acc)
    up, down = tie((above[3], below[3]), acc)
    far_up, far_down = from_z(up[:2], 1), from_z(down[2:], -1)
    acc, g3, g5 = chunk((3, 5), w, rows, [above[3], below[3]], m, acc)
    far = jnp.concatenate([tie(far_up, acc), far_down])
    acc, *g4 = chunk((4,), w, rows, [far], m, acc, split=True)

    def arrive(up, down):
        return [from_z(up[q], -1) for q in p], [from_z(down[q], 1) for q in p]

    def hops(kernel, up_in, down_in, up_own, down_own):
        pairs = [hop(kernel, up_own[q], down_own[q], up_in[q], down_in[q]) for q in p]
        return [x[0] for x in pairs], [x[1] for x in pairs]

    up_in, down_in = from_z(g4[0], -1), from_z(g4[1], 1)
    row_own, *row_sends = row_hop(acc, from_core(acc[1]))
    up, down = first_hop(*tie((up_in, down_in), row_own), g3, g5)
    up_in, down_in = arrive(up, down)
    row_parts = [row_own] + [from_x(row_sends[k - 1], -k) for k in (1, 2, 3)]
    up_in[1], down_in[1] = tie((up_in[1], down_in[1]), *row_parts)
    up, down = hops(hop_kernel, up_in, down_in, g2, g6)
    up, down = hops(hop_kernel, *arrive(up, down), g1, g7)
    up_in, down_in = arrive(up, down)
    own, *sends = last_hop(g0, up_in, down_in)
    return final(*row_parts, own, *[from_y(sends[k - 1], -k) for k in (1, 2, 3)])


def solution(mesh):
    placed = (
        P(("row", "col"), None),
        P(("row", "col")),
        P(("row", "col"), None),
        P(("row", "col"), None),
        P(("row", "col"), None, None, None),
        P(("row", "col"), None),
        P(("row", "col"), None),
        P(("row", "col"), None),
    )
    return jax.shard_map(
        local, mesh=mesh, in_specs=placed, out_specs=P(("row", "col"), None), check_vma=False
    )
```

```python
import functools

import jax
import jax.numpy as jnp
from jax import lax
from jax.experimental import pallas as pl
from jax.experimental.pallas import tpu as pltpu
from jax.sharding import PartitionSpec as P

NY, NZ, NX, NC = 4, 8, 4, 2
T = 128
C = 512
BF = jnp.bfloat16
F32 = jnp.float32
VMEM = pl.BlockSpec(memory_space=pltpu.VMEM)
SMEM = pl.BlockSpec(memory_space=pltpu.SMEM)
PARAMS = pltpu.CompilerParams(vmem_limit_bytes=28 * 1024 * 1024)
SLOTS = 16
BUFFERS = 4
PIECES = ((0, 256), (256, 512))
FAR = NZ // 2


def from_y(x, k):
    perm = [(((y + k) % NY) * NZ + z, y * NZ + z) for y in range(NY) for z in range(NZ)]
    return lax.ppermute(x, "row", perm)


def from_z(x, k):
    perm = [(y * NZ + (z + k) % NZ, y * NZ + z) for y in range(NY) for z in range(NZ)]
    return lax.ppermute(x, "row", perm)


def from_x(x, k):
    perm = [(((s + k) % NX) * NC + c, s * NC + c) for s in range(NX) for c in range(NC)]
    return lax.ppermute(x, "col", perm)


def from_core(x):
    perm = [(s * NC + 1 - c, s * NC + c) for s in range(NX) for c in range(NC)]
    return lax.ppermute(x, "col", perm)


def prep_kernel(ints, nw, masks, m_ref, w_ref, buf, sem):
    n_slots, n_neg = masks.shape[1], nw.shape[1]
    at_neg, at_pos = 2 * n_slots, 2 * (n_slots + n_neg)
    count = ints[at_pos + 4]
    y, z, x, c = ints[at_pos], ints[at_pos + 1], ints[at_pos + 2], ints[at_pos + 3]
    n_blocks = masks.shape[1] // SLOTS

    def fetch(b):
        at = b % BUFFERS
        return pltpu.make_async_copy(masks.at[0, pl.ds(b * SLOTS, SLOTS)], buf.at[at], sem.at[at])

    for b in range(BUFFERS):
        fetch(b).start()

    def row_at(a):
        return ((a % NC) ^ c) * NX + ((a // NC - x) & (NX - 1))

    def col_at(b):
        return (b % NZ - z) & (NZ - 1), (b // NZ - y) & (NY - 1)

    m_ref[...] = jnp.zeros_like(m_ref)

    for a in range(NX * NC):
        for b in range(NY * NZ):
            w_ref[a, b] = 0.0

    def negative(p, _):
        d, e = col_at(ints[at_neg + n_neg + p])
        a = row_at(ints[at_neg + p])
        w_ref[a, d * NY + e] += nw[0, p]
        return 0

    lax.fori_loop(0, n_neg, negative, 0)

    def block(b, _):
        fetch(b).wait()

        def slot(t, _):
            a = row_at(ints[b * SLOTS + t])
            d, e = col_at(ints[n_slots + b * SLOTS + t])
            at = (d, pl.ds(pl.multiple_of(a * T, T), T), pl.ds(pl.multiple_of(e * T, T), T))
            m_ref[at] += buf[b % BUFFERS, t].astype(F32).astype(BF)
            return 0

        lax.fori_loop(0, jnp.clip(count - b * SLOTS, 0, SLOTS), slot, 0)

        @pl.when(b + BUFFERS < n_blocks)
        def _():
            fetch(b + BUFFERS).start()

        return 0

    lax.fori_loop(0, n_blocks, block, 0)


def prep(ints, nw, masks):
    return pl.pallas_call(
        prep_kernel,
        out_shape=(
            jax.ShapeDtypeStruct((NZ, NX * NC * T, NY * T), BF),
            jax.ShapeDtypeStruct((NX * NC, NY * NZ), F32),
        ),
        in_specs=[SMEM, SMEM, pl.BlockSpec(memory_space=pltpu.HBM)],
        out_specs=(VMEM, SMEM),
        scratch_shapes=[pltpu.VMEM((BUFFERS, SLOTS, T, T), jnp.int32), pltpu.SemaphoreType.DMA((BUFFERS,))],
        compiler_params=pltpu.CompilerParams(vmem_limit_bytes=45 * 1024 * 1024),
        cost_estimate=pl.CostEstimate(flops=0, bytes_accessed=16 << 20, transcendentals=0),
        name="prep",
    )(ints, nw, masks)


def dot(a, b, dims):
    return lax.dot_general(a, b, (dims, ((), ())), preferred_element_type=F32)


def row_sums_kernel(r_ref, out):
    def body(h, _):
        for f in range(NX):
            out[h, f : f + 1] = jnp.sum(r_ref[h, f * T : (f + 1) * T].astype(F32), axis=0, keepdims=True)
        return 0

    lax.fori_loop(0, 2, body, 0)


def row_sums(r):
    return pl.pallas_call(
        row_sums_kernel,
        out_shape=jax.ShapeDtypeStruct((2, 8, C), F32),
        in_specs=[VMEM],
        out_specs=VMEM,
        compiler_params=PARAMS,
        name="row_sums",
    )(r)


def chunk_kernel(ds, first, w_ref, r_ref, row_sums, *refs):
    n = len(ds)
    k_refs, refs = refs[:n], refs[n:]
    m_ref, refs = refs[0], refs[1:]
    if not first:
        acc_in, refs = refs[0], refs[1:]
    p = len(PIECES)
    rows_out, refs, (g_acc, k_all, col_sums) = refs[0], refs[1:-3], refs[-3:]

    def begin(e, _):
        at = pl.ds(pl.multiple_of(e * T, T), T)
        for h in range(2):
            rows_out[h, at] = jnp.zeros((T, C), F32) if first else acc_in[h, at]
        for c in range(n):
            k = k_refs[c][e]
            k_all[c, at] = k
            g_acc[c, at] = jnp.zeros((T, C), F32)
            col_sums[c, pl.ds(e, 1)] = jnp.sum(k.astype(F32), axis=0, keepdims=True)
        return 0

    lax.fori_loop(0, NY, begin, 0)

    def body(step, _):
        c, h = step // 2, step % 2
        d = ds[0] if n == 1 else jnp.where(c == 0, ds[0], ds[1])
        x, k = r_ref[h], k_all[c]
        s = dot(x, k, ((1,), (1,)))
        at = pl.ds(pl.multiple_of(h * NX * T, NX * T), NX * T)
        coef = (1.0 / (1.0 - jnp.exp(s))).astype(BF) * m_ref[d, at]
        g = dot(coef, x, ((0,), (0,)))
        r = dot(coef, k, ((1,), (0,)))
        sums = [row_sums[h, f : f + 1] for f in range(NX)]
        weights = [[w_ref[h * NX + f, d * NY + e] for e in range(NY)] for f in range(NX)]
        for e in range(NY):
            v = sum(weights[f][e] * sums[f] for f in range(NX))
            g_acc[c, e * T : (e + 1) * T] += g[e * T : (e + 1) * T] + v
        for f in range(NX):
            v = sum(weights[f][e] * col_sums[c, e : e + 1] for e in range(NY))
            rows = r[f * T : (f + 1) * T] + v
            rows_out[h, f * T : (f + 1) * T] += rows
        return 0

    lax.fori_loop(0, 2 * n, body, 0)

    def end(e, _):
        for c in range(n):
            done = g_acc[c, pl.ds(pl.multiple_of(e * T, T), T)].astype(BF)
            for q, (lo, hi) in enumerate(PIECES):
                refs[c * p + q][e] = done[:, lo:hi]
        return 0

    lax.fori_loop(0, NY, end, 0)


def chunk(ds, w, rows, ks, m, acc):
    n, p = len(ds), len(PIECES)
    first = acc is None
    args = [w, *rows, *ks, m] + ([] if first else [acc])
    shapes = [((2, NX * T, C), F32)]
    shapes += [((NY, T, hi - lo), BF) for _ in ds for lo, hi in PIECES]
    out = pl.pallas_call(
        functools.partial(chunk_kernel, ds, first),
        out_shape=[jax.ShapeDtypeStruct(*s) for s in shapes],
        in_specs=[SMEM] + [VMEM] * (len(args) - 1),
        out_specs=[VMEM] * len(shapes),
        scratch_shapes=[pltpu.VMEM((n, NY * T, C), F32), pltpu.VMEM((n, NY * T, C), BF), pltpu.VMEM((n, 8, C), F32)],
        input_output_aliases={} if first else {len(args) - 1: 0},
        compiler_params=PARAMS,
        cost_estimate=pl.CostEstimate(
            flops=n * 6 * 1024 * 512 * 512, bytes_accessed=(n * 2 + 6) << 20, transcendentals=n * 1024 * 512
        ),
        name="chunk",
    )(*args)
    return out[0], *[out[1 + c * p : 1 + (c + 1) * p] for c in range(n)]


def far_cols_kernel(w_ref, r_ref, row_sums, k_ref, m_ref, g_up, g_down, coef_ref, g_acc):
    g_acc[...] = jnp.zeros_like(g_acc)

    def body(h, _):
        x, k = r_ref[h], k_ref[...].reshape(NY * T, C)
        s = dot(x, k, ((1,), (1,)))
        at = pl.ds(pl.multiple_of(h * NX * T, NX * T), NX * T)
        coef = (1.0 / (1.0 - jnp.exp(s))).astype(BF) * m_ref[FAR, at]
        coef_ref[h] = coef
        g = dot(coef, x, ((0,), (0,)))
        for e in range(NY):
            v = sum(w_ref[h * NX + f, FAR * NY + e] * row_sums[h, f : f + 1] for f in range(NX))
            g_acc[e * T : (e + 1) * T] += g[e * T : (e + 1) * T] + v
        return 0

    lax.fori_loop(0, 2, body, 0)
    for e in range(NY):
        (g_up, g_down)[e // 2][e % 2] = g_acc[e * T : (e + 1) * T].astype(BF)


def far_cols(w, rows, k, m):
    return pl.pallas_call(
        far_cols_kernel,
        out_shape=[jax.ShapeDtypeStruct((2, T, C), BF)] * 2 + [jax.ShapeDtypeStruct((2, NX * T, NY * T), BF)],
        in_specs=[SMEM] + [VMEM] * 4,
        out_specs=[VMEM] * 3,
        scratch_shapes=[pltpu.VMEM((NY * T, C), F32)],
        compiler_params=PARAMS,
        cost_estimate=pl.CostEstimate(flops=4 * 1024 * 512 * 512, bytes_accessed=4 << 20, transcendentals=1024 * 512),
        name="far_cols",
    )(w, *rows, k, m)


def far_rows_kernel(w_ref, coef_ref, k_ref, acc_in, keep, send, col_sums):
    for e in range(NY):
        col_sums[e : e + 1] = jnp.sum(k_ref[e].astype(F32), axis=0, keepdims=True)

    for h in range(2):
        r = dot(coef_ref[h], k_ref[...].reshape(NY * T, C), ((1,), (0,)))
        for f in range(NX):
            v = sum(w_ref[h * NX + f, FAR * NY + e] * col_sums[e : e + 1] for e in range(NY))
            total = r[f * T : (f + 1) * T] + v + acc_in[h, f * T : (f + 1) * T]
            if h:
                send[f] = total.astype(BF)
            else:
                keep[f] = total


def far_rows(w, coef, k, acc):
    return pl.pallas_call(
        far_rows_kernel,
        out_shape=[jax.ShapeDtypeStruct((NX, T, C), F32), jax.ShapeDtypeStruct((NX, T, C), BF)],
        in_specs=[SMEM] + [VMEM] * 3,
        out_specs=[VMEM, VMEM],
        scratch_shapes=[pltpu.VMEM((8, C), F32)],
        compiler_params=PARAMS,
        cost_estimate=pl.CostEstimate(flops=2 * 1024 * 512 * 512, bytes_accessed=8 << 20, transcendentals=0),
        name="far_rows",
    )(w, coef, k, acc)


def first_hop_kernel(up_in, down_in, *refs):
    p = len(PIECES)
    ups, downs, up_outs, down_outs = refs[:p], refs[p : 2 * p], refs[2 * p : 3 * p], refs[3 * p :]
    for q, (lo, hi) in enumerate(PIECES):
        up_outs[q][:2] = (ups[q][:2].astype(F32) + up_in[:, :, lo:hi].astype(F32)).astype(BF)
        up_outs[q][2:] = ups[q][2:]
        down_outs[q][:2] = downs[q][:2]
        down_outs[q][2:] = (downs[q][2:].astype(F32) + down_in[:, :, lo:hi].astype(F32)).astype(BF)


def first_hop(up_in, down_in, ups, downs):
    own = [*ups, *downs]
    out = pl.pallas_call(
        first_hop_kernel,
        out_shape=[jax.ShapeDtypeStruct(x.shape, BF) for x in own],
        in_specs=[VMEM] * (2 + len(own)),
        out_specs=[VMEM] * len(own),
        compiler_params=PARAMS,
        cost_estimate=pl.CostEstimate(flops=1 << 20, bytes_accessed=3 << 20, transcendentals=0),
        name="first_hop",
    )(up_in, down_in, *own)
    return list(out[: len(ups)]), list(out[len(ups) :])


def hop_kernel(up, down, up_in, down_in, up_out, down_out):
    up_out[...] = (up[...].astype(F32) + up_in[...].astype(F32)).astype(BF)
    down_out[...] = (down[...].astype(F32) + down_in[...].astype(F32)).astype(BF)


def hop(kernel, up, down, up_in, down_in):
    return pl.pallas_call(
        kernel,
        out_shape=[jax.ShapeDtypeStruct(up.shape, BF)] * 2,
        in_specs=[VMEM] * 4,
        out_specs=[VMEM] * 2,
        compiler_params=PARAMS,
        cost_estimate=pl.CostEstimate(flops=1 << 20, bytes_accessed=3 << 20, transcendentals=0),
        name="hop",
    )(up, down, up_in, down_in)


def last_hop_kernel(*refs):
    p = len(PIECES)
    keep, *sends = refs[3 * p :]
    for q, (lo, hi) in enumerate(PIECES):
        for e in range(NY):
            s = sum(refs[k * p + q][e].astype(F32) for k in range(3))
            if e:
                sends[e - 1][:, lo:hi] = s.astype(BF)
            else:
                keep[:, lo:hi] = s


def last_hop(own, up_in, down_in):
    args = [*own, *up_in, *down_in]
    return pl.pallas_call(
        last_hop_kernel,
        out_shape=[jax.ShapeDtypeStruct((T, C), F32)] + [jax.ShapeDtypeStruct((T, C), BF)] * (NY - 1),
        in_specs=[VMEM] * len(args),
        out_specs=[VMEM] * NY,
        compiler_params=PARAMS,
        cost_estimate=pl.CostEstimate(flops=1 << 20, bytes_accessed=2 << 20, transcendentals=0),
        name="last_hop",
    )(*args)


def row_hop_kernel(keep, arrived, own, *sends):
    for f in range(NX):
        s = keep[f] + arrived[f].astype(F32)
        if f:
            sends[f - 1][...] = s.astype(BF)
        else:
            own[...] = s


def row_hop(keep, arrived):
    return pl.pallas_call(
        row_hop_kernel,
        out_shape=[jax.ShapeDtypeStruct((T, C), F32)] + [jax.ShapeDtypeStruct((T, C), BF)] * (NX - 1),
        in_specs=[VMEM] * 2,
        out_specs=[VMEM] * NX,
        compiler_params=PARAMS,
        cost_estimate=pl.CostEstimate(flops=1 << 19, bytes_accessed=3 << 20, transcendentals=0),
        name="row_hop",
    )(keep, arrived)


def final_kernel(*refs):
    out = refs[-1]
    total = refs[0][...]
    for part in refs[1:-1]:
        total = total + part[...].astype(F32)
    out[...] = total


def final(*terms):
    return pl.pallas_call(
        final_kernel,
        out_shape=jax.ShapeDtypeStruct((T, C), F32),
        in_specs=[VMEM] * len(terms),
        out_specs=VMEM,
        compiler_params=PARAMS,
        name="final",
    )(*terms)


def tie(x, *tokens):
    return lax.optimization_barrier((x, *tokens))[0]


def local(membership, tile_count, tile_rows, tile_cols, edge_masks, neg_rows, neg_cols, neg_weight):
    i, j = lax.axis_index("row"), lax.axis_index("col")
    pos = jnp.stack([i // NZ, i % NZ, j // NC, j % NC]).astype(jnp.int32)
    ints = jnp.concatenate([tile_rows[0], tile_cols[0], neg_rows[0], neg_cols[0], pos, tile_count])
    shard = membership.astype(BF)
    next_y, last_y = from_y(shard, 1), from_y(shard, -1)
    half = T // 2
    far_y = jnp.concatenate([from_y(next_y[:half], 1), from_y(last_y[half:], -1)])
    stack = [shard, next_y, far_y, last_y]
    first = jnp.stack(stack)
    same = jnp.stack([shard] + [from_x(shard, k) for k in (1, 2, 3)])
    m, w = prep(tie(ints, first), neg_weight, edge_masks)
    same = jnp.stack([shard] + [from_x(shard, k) for k in (1, 2, 3)])
    p = range(len(PIECES))

    above, below = [first], [first]

    def step(*token):
        up, down = tie((above[-1], below[-1]), *token)
        above.append(from_z(up, 1))
        below.append(from_z(down, -1))

    step()
    r = jnp.stack([same, from_core(tie(same, m))]).reshape(2, NX * T, C)
    rows = r, row_sums(r)
    step(m)
    acc, g0 = chunk((0,), tie(w, above[1]), rows, [first], m, None)
    acc, g1, g7 = chunk((1, 7), w, rows, [above[1], below[1]], m, acc)
    step(acc)
    acc, g2, g6 = chunk((2, 6), w, rows, [above[2], below[2]], m, acc)
    up, down = tie((above[3], below[3]), acc)
    far_up, far_down = from_z(up[:2], 1), from_z(down[2:], -1)
    acc, g3, g5 = chunk((3, 5), w, rows, [above[3], below[3]], m, acc)
    far = jnp.concatenate([tie(far_up, acc), far_down])
    *g4, coef = far_cols(w, rows, far, m)

    def arrive(up, down):
        return [from_z(up[q], -1) for q in p], [from_z(down[q], 1) for q in p]

    def hops(kernel, up_in, down_in, up_own, down_own):
        pairs = [hop(kernel, up_own[q], down_own[q], up_in[q], down_in[q]) for q in p]
        return [x[0] for x in pairs], [x[1] for x in pairs]

    up_in, down_in = from_z(g4[0], -1), from_z(g4[1], 1)
    row_keep, row_send = far_rows(w, coef, far, acc)
    row_own, *row_sends = row_hop(row_keep, from_core(row_send))
    up, down = first_hop(up_in, down_in, g3, g5)
    up_in, down_in = arrive(up, down)
    up, down = hops(hop_kernel, up_in, down_in, g2, g6)
    up_in, down_in = arrive(up, down)
    up_in[0], down_in[0] = tie((up_in[0], down_in[0]), row_own)
    up, down = hops(hop_kernel, up_in, down_in, g1, g7)
    up_in, down_in = arrive(up, down)
    row_parts = [row_own] + [from_x(row_sends[k - 1], -k) for k in (1, 2, 3)]
    up_in[1], down_in[1] = tie((up_in[1], down_in[1]), *row_parts)
    own, *sends = last_hop(g0, up_in, down_in)
    return final(*row_parts, own, *[from_y(sends[k - 1], -k) for k in (1, 2, 3)])


def solution(mesh):
    placed = (
        P(("row", "col"), None),
        P(("row", "col")),
        P(("row", "col"), None),
        P(("row", "col"), None),
        P(("row", "col"), None, None, None),
        P(("row", "col"), None),
        P(("row", "col"), None),
        P(("row", "col"), None),
    )
    return jax.shard_map(
        local, mesh=mesh, in_specs=placed, out_specs=P(("row", "col"), None), check_vma=False
    )
```

```python
import functools

import jax
import jax.numpy as jnp
from jax import lax
from jax.experimental import pallas as pl
from jax.experimental.pallas import tpu as pltpu
from jax.sharding import PartitionSpec as P

NY, NZ, NX, NC = 4, 8, 4, 2
T = 128
C = 512
BF = jnp.bfloat16
F32 = jnp.float32
VMEM = pl.BlockSpec(memory_space=pltpu.VMEM)
SMEM = pl.BlockSpec(memory_space=pltpu.SMEM)
PARAMS = pltpu.CompilerParams(vmem_limit_bytes=28 * 1024 * 1024)
SLOTS = 16
BUFFERS = 4
PIECES = ((0, 256), (256, 512))
FAR = NZ // 2


def from_y(x, k):
    perm = [(((y + k) % NY) * NZ + z, y * NZ + z) for y in range(NY) for z in range(NZ)]
    return lax.ppermute(x, "row", perm)


def from_z(x, k):
    perm = [(y * NZ + (z + k) % NZ, y * NZ + z) for y in range(NY) for z in range(NZ)]
    return lax.ppermute(x, "row", perm)


def from_x(x, k):
    perm = [(((s + k) % NX) * NC + c, s * NC + c) for s in range(NX) for c in range(NC)]
    return lax.ppermute(x, "col", perm)


def from_core(x):
    perm = [(s * NC + 1 - c, s * NC + c) for s in range(NX) for c in range(NC)]
    return lax.ppermute(x, "col", perm)


def prep_kernel(ints, nw, masks, m_ref, w_ref, buf, sem):
    n_slots, n_neg = masks.shape[1], nw.shape[1]
    at_neg, at_pos = 2 * n_slots, 2 * (n_slots + n_neg)
    count = ints[at_pos + 4]
    y, z, x, c = ints[at_pos], ints[at_pos + 1], ints[at_pos + 2], ints[at_pos + 3]
    n_blocks = masks.shape[1] // SLOTS

    def fetch(b):
        at = b % BUFFERS
        return pltpu.make_async_copy(masks.at[0, pl.ds(b * SLOTS, SLOTS)], buf.at[at], sem.at[at])

    for b in range(BUFFERS):
        fetch(b).start()

    def row_at(a):
        return ((a % NC) ^ c) * NX + ((a // NC - x) & (NX - 1))

    def col_at(b):
        return (b % NZ - z) & (NZ - 1), (b // NZ - y) & (NY - 1)

    m_ref[...] = jnp.zeros_like(m_ref)

    for a in range(NX * NC):
        for b in range(NY * NZ):
            w_ref[a, b] = 0.0

    def negative(p, _):
        d, e = col_at(ints[at_neg + n_neg + p])
        a = row_at(ints[at_neg + p])
        w_ref[a, d * NY + e] += nw[0, p]
        return 0

    lax.fori_loop(0, n_neg, negative, 0)

    def block(b, _):
        fetch(b).wait()

        def slot(t, _):
            a = row_at(ints[b * SLOTS + t])
            d, e = col_at(ints[n_slots + b * SLOTS + t])
            at = (d, pl.ds(pl.multiple_of(a * T, T), T), pl.ds(pl.multiple_of(e * T, T), T))
            m_ref[at] += buf[b % BUFFERS, t].astype(F32).astype(BF)
            return 0

        lax.fori_loop(0, jnp.clip(count - b * SLOTS, 0, SLOTS), slot, 0)

        @pl.when(b + BUFFERS < n_blocks)
        def _():
            fetch(b + BUFFERS).start()

        return 0

    lax.fori_loop(0, n_blocks, block, 0)


def prep(ints, nw, masks):
    return pl.pallas_call(
        prep_kernel,
        out_shape=(
            jax.ShapeDtypeStruct((NZ, NX * NC * T, NY * T), BF),
            jax.ShapeDtypeStruct((NX * NC, NY * NZ), F32),
        ),
        in_specs=[SMEM, SMEM, pl.BlockSpec(memory_space=pltpu.HBM)],
        out_specs=(VMEM, SMEM),
        scratch_shapes=[pltpu.VMEM((BUFFERS, SLOTS, T, T), jnp.int32), pltpu.SemaphoreType.DMA((BUFFERS,))],
        compiler_params=pltpu.CompilerParams(vmem_limit_bytes=45 * 1024 * 1024),
        cost_estimate=pl.CostEstimate(flops=0, bytes_accessed=16 << 20, transcendentals=0),
        name="prep",
    )(ints, nw, masks)


def dot(a, b, dims):
    return lax.dot_general(a, b, (dims, ((), ())), preferred_element_type=F32)


def row_sums_kernel(r_ref, out):
    def body(h, _):
        for f in range(NX):
            out[h, f : f + 1] = jnp.sum(r_ref[h, f * T : (f + 1) * T].astype(F32), axis=0, keepdims=True)
        return 0

    lax.fori_loop(0, 2, body, 0)


def row_sums(r):
    return pl.pallas_call(
        row_sums_kernel,
        out_shape=jax.ShapeDtypeStruct((2, 8, C), F32),
        in_specs=[VMEM],
        out_specs=VMEM,
        compiler_params=PARAMS,
        name="row_sums",
    )(r)


def chunk_kernel(ds, first, w_ref, r_ref, row_sums, *refs):
    n = len(ds)
    k_refs, refs = refs[:n], refs[n:]
    m_ref, refs = refs[0], refs[1:]
    if not first:
        acc_in, refs = refs[0], refs[1:]
    p = len(PIECES)
    rows_out, refs, (g_acc, k_all, col_sums) = refs[0], refs[1:-3], refs[-3:]

    def begin(e, _):
        at = pl.ds(pl.multiple_of(e * T, T), T)
        for h in range(2):
            rows_out[h, at] = jnp.zeros((T, C), F32) if first else acc_in[h, at]
        for c in range(n):
            k = k_refs[c][e]
            k_all[c, at] = k
            g_acc[c, at] = jnp.zeros((T, C), F32)
            col_sums[c, pl.ds(e, 1)] = jnp.sum(k.astype(F32), axis=0, keepdims=True)
        return 0

    lax.fori_loop(0, NY, begin, 0)

    def body(step, _):
        c, h = step // 2, step % 2
        d = ds[0] if n == 1 else jnp.where(c == 0, ds[0], ds[1])
        x, k = r_ref[h], k_all[c]
        s = dot(x, k, ((1,), (1,)))
        at = pl.ds(pl.multiple_of(h * NX * T, NX * T), NX * T)
        coef = (1.0 / (1.0 - jnp.exp(s))).astype(BF) * m_ref[d, at]
        g = dot(coef, x, ((0,), (0,)))
        r = dot(coef, k, ((1,), (0,)))
        sums = [row_sums[h, f : f + 1] for f in range(NX)]
        weights = [[w_ref[h * NX + f, d * NY + e] for e in range(NY)] for f in range(NX)]
        for e in range(NY):
            v = sum(weights[f][e] * sums[f] for f in range(NX))
            g_acc[c, e * T : (e + 1) * T] += g[e * T : (e + 1) * T] + v
        for f in range(NX):
            v = sum(weights[f][e] * col_sums[c, e : e + 1] for e in range(NY))
            rows = r[f * T : (f + 1) * T] + v
            rows_out[h, f * T : (f + 1) * T] += rows
        return 0

    lax.fori_loop(0, 2 * n, body, 0)

    def end(e, _):
        for c in range(n):
            done = g_acc[c, pl.ds(pl.multiple_of(e * T, T), T)].astype(BF)
            for q, (lo, hi) in enumerate(PIECES):
                refs[c * p + q][e] = done[:, lo:hi]
        return 0

    lax.fori_loop(0, NY, end, 0)


def chunk(ds, w, rows, ks, m, acc):
    n, p = len(ds), len(PIECES)
    first = acc is None
    args = [w, *rows, *ks, m] + ([] if first else [acc])
    shapes = [((2, NX * T, C), F32)]
    shapes += [((NY, T, hi - lo), BF) for _ in ds for lo, hi in PIECES]
    out = pl.pallas_call(
        functools.partial(chunk_kernel, ds, first),
        out_shape=[jax.ShapeDtypeStruct(*s) for s in shapes],
        in_specs=[SMEM] + [VMEM] * (len(args) - 1),
        out_specs=[VMEM] * len(shapes),
        scratch_shapes=[pltpu.VMEM((n, NY * T, C), F32), pltpu.VMEM((n, NY * T, C), BF), pltpu.VMEM((n, 8, C), F32)],
        input_output_aliases={} if first else {len(args) - 1: 0},
        compiler_params=PARAMS,
        cost_estimate=pl.CostEstimate(
            flops=n * 6 * 1024 * 512 * 512, bytes_accessed=(n * 2 + 6) << 20, transcendentals=n * 1024 * 512
        ),
        name="chunk",
    )(*args)
    return out[0], *[out[1 + c * p : 1 + (c + 1) * p] for c in range(n)]


def far_cols_kernel(w_ref, r_ref, row_sums, k_ref, m_ref, g_up, g_down, coef_ref, g_acc):
    g_acc[...] = jnp.zeros_like(g_acc)

    def body(h, _):
        x, k = r_ref[h], k_ref[...].reshape(NY * T, C)
        s = dot(x, k, ((1,), (1,)))
        at = pl.ds(pl.multiple_of(h * NX * T, NX * T), NX * T)
        coef = (1.0 / (1.0 - jnp.exp(s))).astype(BF) * m_ref[FAR, at]
        coef_ref[h] = coef
        g = dot(coef, x, ((0,), (0,)))
        for e in range(NY):
            v = sum(w_ref[h * NX + f, FAR * NY + e] * row_sums[h, f : f + 1] for f in range(NX))
            g_acc[e * T : (e + 1) * T] += g[e * T : (e + 1) * T] + v
        return 0

    lax.fori_loop(0, 2, body, 0)
    for e in range(NY):
        (g_up, g_down)[e // 2][e % 2] = g_acc[e * T : (e + 1) * T].astype(BF)


def far_cols(w, rows, k, m):
    return pl.pallas_call(
        far_cols_kernel,
        out_shape=[jax.ShapeDtypeStruct((2, T, C), BF)] * 2 + [jax.ShapeDtypeStruct((2, NX * T, NY * T), BF)],
        in_specs=[SMEM] + [VMEM] * 4,
        out_specs=[VMEM] * 3,
        scratch_shapes=[pltpu.VMEM((NY * T, C), F32)],
        compiler_params=PARAMS,
        cost_estimate=pl.CostEstimate(flops=4 * 1024 * 512 * 512, bytes_accessed=4 << 20, transcendentals=1024 * 512),
        name="far_cols",
    )(w, *rows, k, m)


def far_rows_kernel(w_ref, coef_ref, k_ref, acc_in, keep, send, col_sums):
    for e in range(NY):
        col_sums[e : e + 1] = jnp.sum(k_ref[e].astype(F32), axis=0, keepdims=True)

    for h in range(2):
        r = dot(coef_ref[h], k_ref[...].reshape(NY * T, C), ((1,), (0,)))
        for f in range(NX):
            v = sum(w_ref[h * NX + f, FAR * NY + e] * col_sums[e : e + 1] for e in range(NY))
            total = r[f * T : (f + 1) * T] + v + acc_in[h, f * T : (f + 1) * T]
            if h:
                send[f] = total.astype(BF)
            else:
                keep[f] = total


def far_rows(w, coef, k, acc):
    return pl.pallas_call(
        far_rows_kernel,
        out_shape=[jax.ShapeDtypeStruct((NX, T, C), F32), jax.ShapeDtypeStruct((NX, T, C), BF)],
        in_specs=[SMEM] + [VMEM] * 3,
        out_specs=[VMEM, VMEM],
        scratch_shapes=[pltpu.VMEM((8, C), F32)],
        compiler_params=PARAMS,
        cost_estimate=pl.CostEstimate(flops=2 * 1024 * 512 * 512, bytes_accessed=8 << 20, transcendentals=0),
        name="far_rows",
    )(w, coef, k, acc)


def first_hop_kernel(up_in, down_in, *refs):
    p = len(PIECES)
    ups, downs, up_outs, down_outs = refs[:p], refs[p : 2 * p], refs[2 * p : 3 * p], refs[3 * p :]
    for q, (lo, hi) in enumerate(PIECES):
        up_outs[q][:2] = (ups[q][:2].astype(F32) + up_in[:, :, lo:hi].astype(F32)).astype(BF)
        up_outs[q][2:] = ups[q][2:]
        down_outs[q][:2] = downs[q][:2]
        down_outs[q][2:] = (downs[q][2:].astype(F32) + down_in[:, :, lo:hi].astype(F32)).astype(BF)


def first_hop(up_in, down_in, ups, downs):
    own = [*ups, *downs]
    out = pl.pallas_call(
        first_hop_kernel,
        out_shape=[jax.ShapeDtypeStruct(x.shape, BF) for x in own],
        in_specs=[VMEM] * (2 + len(own)),
        out_specs=[VMEM] * len(own),
        compiler_params=PARAMS,
        cost_estimate=pl.CostEstimate(flops=1 << 20, bytes_accessed=3 << 20, transcendentals=0),
        name="first_hop",
    )(up_in, down_in, *own)
    return list(out[: len(ups)]), list(out[len(ups) :])


def hop_kernel(up, down, up_in, down_in, up_out, down_out):
    up_out[...] = (up[...].astype(F32) + up_in[...].astype(F32)).astype(BF)
    down_out[...] = (down[...].astype(F32) + down_in[...].astype(F32)).astype(BF)


def hop(kernel, up, down, up_in, down_in):
    return pl.pallas_call(
        kernel,
        out_shape=[jax.ShapeDtypeStruct(up.shape, BF)] * 2,
        in_specs=[VMEM] * 4,
        out_specs=[VMEM] * 2,
        compiler_params=PARAMS,
        cost_estimate=pl.CostEstimate(flops=1 << 20, bytes_accessed=3 << 20, transcendentals=0),
        name="hop",
    )(up, down, up_in, down_in)


def last_hop_kernel(*refs):
    p = len(PIECES)
    keep, *sends = refs[3 * p :]
    for q, (lo, hi) in enumerate(PIECES):
        for e in range(NY):
            s = sum(refs[k * p + q][e].astype(F32) for k in range(3))
            if e:
                sends[e - 1][:, lo:hi] = s.astype(BF)
            else:
                keep[:, lo:hi] = s


def last_hop(own, up_in, down_in):
    args = [*own, *up_in, *down_in]
    return pl.pallas_call(
        last_hop_kernel,
        out_shape=[jax.ShapeDtypeStruct((T, C), F32)] + [jax.ShapeDtypeStruct((T, C), BF)] * (NY - 1),
        in_specs=[VMEM] * len(args),
        out_specs=[VMEM] * NY,
        compiler_params=PARAMS,
        cost_estimate=pl.CostEstimate(flops=1 << 20, bytes_accessed=2 << 20, transcendentals=0),
        name="last_hop",
    )(*args)


def row_hop_kernel(keep, arrived, own, *sends):
    for f in range(NX):
        s = keep[f] + arrived[f].astype(F32)
        if f:
            sends[f - 1][...] = s.astype(BF)
        else:
            own[...] = s


def row_hop(keep, arrived):
    return pl.pallas_call(
        row_hop_kernel,
        out_shape=[jax.ShapeDtypeStruct((T, C), F32)] + [jax.ShapeDtypeStruct((T, C), BF)] * (NX - 1),
        in_specs=[VMEM] * 2,
        out_specs=[VMEM] * NX,
        compiler_params=PARAMS,
        cost_estimate=pl.CostEstimate(flops=1 << 19, bytes_accessed=3 << 20, transcendentals=0),
        name="row_hop",
    )(keep, arrived)


def final_kernel(*refs):
    out = refs[-1]
    total = refs[0][...]
    for part in refs[1:-1]:
        total = total + part[...].astype(F32)
    out[...] = total


def final(*terms):
    return pl.pallas_call(
        final_kernel,
        out_shape=jax.ShapeDtypeStruct((T, C), F32),
        in_specs=[VMEM] * len(terms),
        out_specs=VMEM,
        compiler_params=PARAMS,
        name="final",
    )(*terms)


def tie(x, *tokens):
    return lax.optimization_barrier((x, *tokens))[0]


def local(membership, tile_count, tile_rows, tile_cols, edge_masks, neg_rows, neg_cols, neg_weight):
    i, j = lax.axis_index("row"), lax.axis_index("col")
    pos = jnp.stack([i // NZ, i % NZ, j // NC, j % NC]).astype(jnp.int32)
    ints = jnp.concatenate([tile_rows[0], tile_cols[0], neg_rows[0], neg_cols[0], pos, tile_count])
    shard = membership.astype(BF)
    next_y, last_y = from_y(shard, 1), from_y(shard, -1)
    half = T // 2
    far_y = jnp.concatenate([from_y(next_y[:half], 1), from_y(last_y[half:], -1)])
    stack = [shard, next_y, far_y, last_y]
    first = jnp.stack(stack)
    same = jnp.stack([shard] + [from_x(shard, k) for k in (1, 2, 3)])
    m, w = prep(tie(ints, first), neg_weight, edge_masks)
    p = range(len(PIECES))

    above, below = [first], [first]

    def step(*token):
        up, down = tie((above[-1], below[-1]), *token)
        above.append(from_z(up, 1))
        below.append(from_z(down, -1))

    step()
    r = jnp.stack([same, from_core(tie(same, m))]).reshape(2, NX * T, C)
    rows = r, row_sums(r)
    step(m)
    acc, g0 = chunk((0,), tie(w, above[1]), rows, [first], m, None)
    acc, g1, g7 = chunk((1, 7), w, rows, [above[1], below[1]], m, acc)
    step(acc)
    acc, g2, g6 = chunk((2, 6), w, rows, [above[2], below[2]], m, acc)
    up, down = tie((above[3], below[3]), acc)
    far_up, far_down = from_z(up[:2], 1), from_z(down[2:], -1)
    acc, g3, g5 = chunk((3, 5), w, rows, [above[3], below[3]], m, acc)
    far = jnp.concatenate([tie(far_up, acc), far_down])
    *g4, coef = far_cols(w, rows, far, m)

    def arrive(up, down):
        return [from_z(up[q], -1) for q in p], [from_z(down[q], 1) for q in p]

    def hops(kernel, up_in, down_in, up_own, down_own):
        pairs = [hop(kernel, up_own[q], down_own[q], up_in[q], down_in[q]) for q in p]
        return [x[0] for x in pairs], [x[1] for x in pairs]

    up_in, down_in = from_z(g4[0], -1), from_z(g4[1], 1)
    row_keep, row_send = far_rows(w, coef, far, acc)
    row_own, *row_sends = row_hop(row_keep, from_core(row_send))
    up, down = first_hop(up_in, down_in, g3, g5)
    up_in, down_in = arrive(up, down)
    up_in[1], down_in[1] = tie((up_in[1], down_in[1]), row_own)
    up, down = hops(hop_kernel, up_in, down_in, g2, g6)
    up_in, down_in = arrive(up, down)
    row_parts = [row_own] + [from_x(row_sends[k - 1], -k) for k in (1, 2, 3)]
    up_in[1], down_in[1] = tie((up_in[1], down_in[1]), *row_parts)
    up, down = hops(hop_kernel, up_in, down_in, g1, g7)
    up_in, down_in = arrive(up, down)
    own, *sends = last_hop(g0, up_in, down_in)
    return final(*row_parts, own, *[from_y(sends[k - 1], -k) for k in (2, 1, 3)])


def solution(mesh):
    placed = (
        P(("row", "col"), None),
        P(("row", "col")),
        P(("row", "col"), None),
        P(("row", "col"), None),
        P(("row", "col"), None, None, None),
        P(("row", "col"), None),
        P(("row", "col"), None),
        P(("row", "col"), None),
    )
    return jax.shard_map(
        local, mesh=mesh, in_specs=placed, out_specs=P(("row", "col"), None), check_vma=False
    )
```

```python
import functools

import jax
import jax.numpy as jnp
from jax import lax
from jax.experimental import pallas as pl
from jax.experimental.pallas import tpu as pltpu
from jax.sharding import PartitionSpec as P

NY, NZ, NX, NC = 4, 8, 4, 2
T = 128
C = 512
BF = jnp.bfloat16
F32 = jnp.float32
VMEM = pl.BlockSpec(memory_space=pltpu.VMEM)
SMEM = pl.BlockSpec(memory_space=pltpu.SMEM)
PARAMS = pltpu.CompilerParams(vmem_limit_bytes=28 * 1024 * 1024)
SLOTS = 16
BUFFERS = 4
PIECES = ((0, 256), (256, 512))
FAR = NZ // 2


def from_y(x, k):
    perm = [(((y + k) % NY) * NZ + z, y * NZ + z) for y in range(NY) for z in range(NZ)]
    return lax.ppermute(x, "row", perm)


def from_z(x, k):
    perm = [(y * NZ + (z + k) % NZ, y * NZ + z) for y in range(NY) for z in range(NZ)]
    return lax.ppermute(x, "row", perm)


def from_x(x, k):
    perm = [(((s + k) % NX) * NC + c, s * NC + c) for s in range(NX) for c in range(NC)]
    return lax.ppermute(x, "col", perm)


def from_core(x):
    perm = [(s * NC + 1 - c, s * NC + c) for s in range(NX) for c in range(NC)]
    return lax.ppermute(x, "col", perm)


def prep_kernel(ints, nw, masks, m_ref, w_ref, buf, sem):
    n_slots, n_neg = masks.shape[1], nw.shape[1]
    at_neg, at_pos = 2 * n_slots, 2 * (n_slots + n_neg)
    count = ints[at_pos + 4]
    y, z, x, c = ints[at_pos], ints[at_pos + 1], ints[at_pos + 2], ints[at_pos + 3]
    n_blocks = masks.shape[1] // SLOTS

    def fetch(b):
        at = b % BUFFERS
        return pltpu.make_async_copy(masks.at[0, pl.ds(b * SLOTS, SLOTS)], buf.at[at], sem.at[at])

    for b in range(BUFFERS):
        fetch(b).start()

    def row_at(a):
        return ((a % NC) ^ c) * NX + ((a // NC - x) & (NX - 1))

    def col_at(b):
        return (b % NZ - z) & (NZ - 1), (b // NZ - y) & (NY - 1)

    def clear(k, _):
        m_ref[k // 8, pl.ds(pl.multiple_of(k % 8 * T, T), T)] = jnp.zeros((T, NY * T), BF)
        return 0

    lax.fori_loop(0, NZ * NX * NC, clear, 0)

    for a in range(NX * NC):
        for b in range(NY * NZ):
            w_ref[a, b] = 0.0

    def negative(p, _):
        d, e = col_at(ints[at_neg + n_neg + p])
        a = row_at(ints[at_neg + p])
        w_ref[a, d * NY + e] += nw[0, p]
        return 0

    lax.fori_loop(0, n_neg, negative, 0)

    def block(b, _):
        fetch(b).wait()

        def slot(t, _):
            a = row_at(ints[b * SLOTS + t])
            d, e = col_at(ints[n_slots + b * SLOTS + t])
            at = (d, pl.ds(pl.multiple_of(a * T, T), T), pl.ds(pl.multiple_of(e * T, T), T))
            m_ref[at] += buf[b % BUFFERS, t].astype(F32).astype(BF)
            return 0

        lax.fori_loop(0, jnp.clip(count - b * SLOTS, 0, SLOTS), slot, 0)

        @pl.when(b + BUFFERS < n_blocks)
        def _():
            fetch(b + BUFFERS).start()

        return 0

    lax.fori_loop(0, n_blocks, block, 0)


def prep(ints, nw, masks):
    return pl.pallas_call(
        prep_kernel,
        out_shape=(
            jax.ShapeDtypeStruct((NZ, NX * NC * T, NY * T), BF),
            jax.ShapeDtypeStruct((NX * NC, NY * NZ), F32),
        ),
        in_specs=[SMEM, SMEM, pl.BlockSpec(memory_space=pltpu.HBM)],
        out_specs=(VMEM, SMEM),
        scratch_shapes=[pltpu.VMEM((BUFFERS, SLOTS, T, T), jnp.int32), pltpu.SemaphoreType.DMA((BUFFERS,))],
        compiler_params=pltpu.CompilerParams(vmem_limit_bytes=45 * 1024 * 1024),
        cost_estimate=pl.CostEstimate(flops=0, bytes_accessed=16 << 20, transcendentals=0),
        name="prep",
    )(ints, nw, masks)


def dot(a, b, dims):
    return lax.dot_general(a, b, (dims, ((), ())), preferred_element_type=F32)


def row_sums_kernel(r_ref, out):
    def body(h, _):
        for f in range(NX):
            out[h, f : f + 1] = jnp.sum(r_ref[h, f * T : (f + 1) * T].astype(F32), axis=0, keepdims=True)
        return 0

    lax.fori_loop(0, 2, body, 0)


def row_sums(r):
    return pl.pallas_call(
        row_sums_kernel,
        out_shape=jax.ShapeDtypeStruct((2, 8, C), F32),
        in_specs=[VMEM],
        out_specs=VMEM,
        compiler_params=PARAMS,
        name="row_sums",
    )(r)


def chunk_kernel(ds, first, w_ref, r_ref, row_sums, *refs):
    n = len(ds)
    k_refs, refs = refs[:n], refs[n:]
    m_ref, refs = refs[0], refs[1:]
    if not first:
        acc_in, refs = refs[0], refs[1:]
    p = len(PIECES)
    rows_out, refs, (g_acc, k_all, col_sums) = refs[0], refs[1:-3], refs[-3:]

    def begin(e, _):
        at = pl.ds(pl.multiple_of(e * T, T), T)
        for h in range(2):
            rows_out[h, at] = jnp.zeros((T, C), F32) if first else acc_in[h, at]
        for c in range(n):
            k = k_refs[c][e]
            k_all[c, at] = k
            g_acc[c, at] = jnp.zeros((T, C), F32)
            col_sums[c, pl.ds(e, 1)] = jnp.sum(k.astype(F32), axis=0, keepdims=True)
        return 0

    lax.fori_loop(0, NY, begin, 0)

    def body(step, _):
        c, h = step // 2, step % 2
        d = ds[0] if n == 1 else jnp.where(c == 0, ds[0], ds[1])
        x, k = r_ref[h], k_all[c]
        s = dot(x, k, ((1,), (1,)))
        at = pl.ds(pl.multiple_of(h * NX * T, NX * T), NX * T)
        coef = (1.0 / (1.0 - jnp.exp(s))).astype(BF) * m_ref[d, at]
        g = dot(coef, x, ((0,), (0,)))
        r = dot(coef, k, ((1,), (0,)))
        sums = [row_sums[h, f : f + 1] for f in range(NX)]
        weights = [[w_ref[h * NX + f, d * NY + e] for e in range(NY)] for f in range(NX)]
        for e in range(NY):
            v = sum(weights[f][e] * sums[f] for f in range(NX))
            g_acc[c, e * T : (e + 1) * T] += g[e * T : (e + 1) * T] + v
        for f in range(NX):
            v = sum(weights[f][e] * col_sums[c, e : e + 1] for e in range(NY))
            rows = r[f * T : (f + 1) * T] + v
            rows_out[h, f * T : (f + 1) * T] += rows
        return 0

    lax.fori_loop(0, 2 * n, body, 0)

    def end(e, _):
        for c in range(n):
            done = g_acc[c, pl.ds(pl.multiple_of(e * T, T), T)].astype(BF)
            for q, (lo, hi) in enumerate(PIECES):
                refs[c * p + q][e] = done[:, lo:hi]
        return 0

    lax.fori_loop(0, NY, end, 0)


def chunk(ds, w, rows, ks, m, acc):
    n, p = len(ds), len(PIECES)
    first = acc is None
    args = [w, *rows, *ks, m] + ([] if first else [acc])
    shapes = [((2, NX * T, C), F32)]
    shapes += [((NY, T, hi - lo), BF) for _ in ds for lo, hi in PIECES]
    out = pl.pallas_call(
        functools.partial(chunk_kernel, ds, first),
        out_shape=[jax.ShapeDtypeStruct(*s) for s in shapes],
        in_specs=[SMEM] + [VMEM] * (len(args) - 1),
        out_specs=[VMEM] * len(shapes),
        scratch_shapes=[pltpu.VMEM((n, NY * T, C), F32), pltpu.VMEM((n, NY * T, C), BF), pltpu.VMEM((n, 8, C), F32)],
        input_output_aliases={} if first else {len(args) - 1: 0},
        compiler_params=PARAMS,
        cost_estimate=pl.CostEstimate(
            flops=n * 6 * 1024 * 512 * 512, bytes_accessed=(n * 2 + 6) << 20, transcendentals=n * 1024 * 512
        ),
        name="chunk",
    )(*args)
    return out[0], *[out[1 + c * p : 1 + (c + 1) * p] for c in range(n)]


def far_cols_kernel(w_ref, r_ref, row_sums, k_ref, m_ref, g_up, g_down, coef_ref, g_acc):
    g_acc[...] = jnp.zeros_like(g_acc)

    def body(h, _):
        x, k = r_ref[h], k_ref[...].reshape(NY * T, C)
        s = dot(x, k, ((1,), (1,)))
        at = pl.ds(pl.multiple_of(h * NX * T, NX * T), NX * T)
        coef = (1.0 / (1.0 - jnp.exp(s))).astype(BF) * m_ref[FAR, at]
        coef_ref[h] = coef
        g = dot(coef, x, ((0,), (0,)))
        for e in range(NY):
            v = sum(w_ref[h * NX + f, FAR * NY + e] * row_sums[h, f : f + 1] for f in range(NX))
            g_acc[e * T : (e + 1) * T] += g[e * T : (e + 1) * T] + v
        return 0

    lax.fori_loop(0, 2, body, 0)
    for e in range(NY):
        (g_up, g_down)[e // 2][e % 2] = g_acc[e * T : (e + 1) * T].astype(BF)


def far_cols(w, rows, k, m):
    return pl.pallas_call(
        far_cols_kernel,
        out_shape=[jax.ShapeDtypeStruct((2, T, C), BF)] * 2 + [jax.ShapeDtypeStruct((2, NX * T, NY * T), BF)],
        in_specs=[SMEM] + [VMEM] * 4,
        out_specs=[VMEM] * 3,
        scratch_shapes=[pltpu.VMEM((NY * T, C), F32)],
        compiler_params=PARAMS,
        cost_estimate=pl.CostEstimate(flops=4 * 1024 * 512 * 512, bytes_accessed=4 << 20, transcendentals=1024 * 512),
        name="far_cols",
    )(w, *rows, k, m)


def far_rows_kernel(w_ref, coef_ref, k_ref, acc_in, keep, send, col_sums):
    for e in range(NY):
        col_sums[e : e + 1] = jnp.sum(k_ref[e].astype(F32), axis=0, keepdims=True)

    for h in range(2):
        r = dot(coef_ref[h], k_ref[...].reshape(NY * T, C), ((1,), (0,)))
        for f in range(NX):
            v = sum(w_ref[h * NX + f, FAR * NY + e] * col_sums[e : e + 1] for e in range(NY))
            total = r[f * T : (f + 1) * T] + v + acc_in[h, f * T : (f + 1) * T]
            if h:
                send[f] = total.astype(BF)
            else:
                keep[f] = total


def far_rows(w, coef, k, acc):
    return pl.pallas_call(
        far_rows_kernel,
        out_shape=[jax.ShapeDtypeStruct((NX, T, C), F32), jax.ShapeDtypeStruct((NX, T, C), BF)],
        in_specs=[SMEM] + [VMEM] * 3,
        out_specs=[VMEM, VMEM],
        scratch_shapes=[pltpu.VMEM((8, C), F32)],
        compiler_params=PARAMS,
        cost_estimate=pl.CostEstimate(flops=2 * 1024 * 512 * 512, bytes_accessed=8 << 20, transcendentals=0),
        name="far_rows",
    )(w, coef, k, acc)


def first_hop_kernel(up_in, down_in, *refs):
    p = len(PIECES)
    ups, downs, up_outs, down_outs = refs[:p], refs[p : 2 * p], refs[2 * p : 3 * p], refs[3 * p :]
    for q, (lo, hi) in enumerate(PIECES):
        up_outs[q][:2] = (ups[q][:2].astype(F32) + up_in[:, :, lo:hi].astype(F32)).astype(BF)
        up_outs[q][2:] = ups[q][2:]
        down_outs[q][:2] = downs[q][:2]
        down_outs[q][2:] = (downs[q][2:].astype(F32) + down_in[:, :, lo:hi].astype(F32)).astype(BF)


def first_hop(up_in, down_in, ups, downs):
    own = [*ups, *downs]
    out = pl.pallas_call(
        first_hop_kernel,
        out_shape=[jax.ShapeDtypeStruct(x.shape, BF) for x in own],
        in_specs=[VMEM] * (2 + len(own)),
        out_specs=[VMEM] * len(own),
        compiler_params=PARAMS,
        cost_estimate=pl.CostEstimate(flops=1 << 20, bytes_accessed=3 << 20, transcendentals=0),
        name="first_hop",
    )(up_in, down_in, *own)
    return list(out[: len(ups)]), list(out[len(ups) :])


def hop_kernel(up, down, up_in, down_in, up_out, down_out):
    up_out[...] = (up[...].astype(F32) + up_in[...].astype(F32)).astype(BF)
    down_out[...] = (down[...].astype(F32) + down_in[...].astype(F32)).astype(BF)


def hop(kernel, up, down, up_in, down_in):
    return pl.pallas_call(
        kernel,
        out_shape=[jax.ShapeDtypeStruct(up.shape, BF)] * 2,
        in_specs=[VMEM] * 4,
        out_specs=[VMEM] * 2,
        compiler_params=PARAMS,
        cost_estimate=pl.CostEstimate(flops=1 << 20, bytes_accessed=3 << 20, transcendentals=0),
        name="hop",
    )(up, down, up_in, down_in)


def last_hop_kernel(own, up_in, down_in, keep, *sends):
    for e in range(NY):
        s = own[e].astype(F32) + up_in[e].astype(F32) + down_in[e].astype(F32)
        if e:
            sends[e - 1][...] = s.astype(BF)
        else:
            keep[...] = s


def last_hop(own, up_in, down_in):
    shape = own.shape[1:]
    return pl.pallas_call(
        last_hop_kernel,
        out_shape=[jax.ShapeDtypeStruct(shape, F32)] + [jax.ShapeDtypeStruct(shape, BF)] * (NY - 1),
        in_specs=[VMEM] * 3,
        out_specs=[VMEM] * NY,
        compiler_params=PARAMS,
        cost_estimate=pl.CostEstimate(flops=1 << 20, bytes_accessed=2 << 20, transcendentals=0),
        name="last_hop",
    )(own, up_in, down_in)


def row_hop_kernel(keep, arrived, own, *sends):
    for f in range(NX):
        s = keep[f] + arrived[f].astype(F32)
        if f:
            sends[f - 1][...] = s.astype(BF)
        else:
            own[...] = s


def row_hop(keep, arrived):
    return pl.pallas_call(
        row_hop_kernel,
        out_shape=[jax.ShapeDtypeStruct((T, C), F32)] + [jax.ShapeDtypeStruct((T, C), BF)] * (NX - 1),
        in_specs=[VMEM] * 2,
        out_specs=[VMEM] * NX,
        compiler_params=PARAMS,
        cost_estimate=pl.CostEstimate(flops=1 << 19, bytes_accessed=3 << 20, transcendentals=0),
        name="row_hop",
    )(keep, arrived)


def final_kernel(*refs):
    out = refs[-1]
    rows = refs[0][...]
    for part in refs[1:NX]:
        rows = rows + part[...].astype(F32)
    for q, (lo, hi) in enumerate(PIECES):
        own, *sent = refs[NX + q * NY : NX + (q + 1) * NY]
        cols = own[...]
        for part in sent:
            cols = cols + part[...].astype(F32)
        out[:, lo:hi] = rows[:, lo:hi] + cols


def final(*terms):
    return pl.pallas_call(
        final_kernel,
        out_shape=jax.ShapeDtypeStruct((T, C), F32),
        in_specs=[VMEM] * len(terms),
        out_specs=VMEM,
        compiler_params=PARAMS,
        name="final",
    )(*terms)


def tie(x, *tokens):
    return lax.optimization_barrier((x, *tokens))[0]


def local(membership, tile_count, tile_rows, tile_cols, edge_masks, neg_rows, neg_cols, neg_weight):
    i, j = lax.axis_index("row"), lax.axis_index("col")
    pos = jnp.stack([i // NZ, i % NZ, j // NC, j % NC]).astype(jnp.int32)
    ints = jnp.concatenate([tile_rows[0], tile_cols[0], neg_rows[0], neg_cols[0], pos, tile_count])
    shard = membership.astype(BF)
    next_y, last_y = from_y(shard, 1), from_y(shard, -1)
    far_y = from_y(next_y, 1)
    stack = [shard, next_y, far_y, last_y]
    first = jnp.stack(stack)
    same = jnp.stack([shard] + [from_x(shard, k) for k in (1, 2, 3)])
    m, w = prep(tie(ints, first), neg_weight, edge_masks)
    p = range(len(PIECES))

    above, below = [first], [first]

    def step(*token):
        up, down = tie((above[-1], below[-1]), *token)
        above.append(from_z(up, 1))
        below.append(from_z(down, -1))

    step()
    r = jnp.stack([same, from_core(tie(same, m))]).reshape(2, NX * T, C)
    rows = r, row_sums(r)
    step(m)
    acc, g0 = chunk((0,), tie(w, above[1]), rows, [first], m, None)
    acc, g1, g7 = chunk((1, 7), w, rows, [above[1], below[1]], m, acc)
    step(acc)
    acc, g2, g6 = chunk((2, 6), w, rows, [above[2], below[2]], m, acc)
    up, down = tie((above[3], below[3]), acc)
    far_up, far_down = from_z(up[:2], 1), from_z(down[2:], -1)
    acc, g3, g5 = chunk((3, 5), w, rows, [above[3], below[3]], m, acc)
    far = jnp.concatenate([tie(far_up, acc), far_down])
    *g4, coef = far_cols(w, rows, far, m)

    def arrive(up, down):
        return [from_z(up[q], -1) for q in p], [from_z(down[q], 1) for q in p]

    def hops(kernel, up_in, down_in, up_own, down_own):
        pairs = [hop(kernel, up_own[q], down_own[q], up_in[q], down_in[q]) for q in p]
        return [x[0] for x in pairs], [x[1] for x in pairs]

    up_in, down_in = from_z(g4[0], -1), from_z(g4[1], 1)
    row_keep, row_send = far_rows(w, coef, far, acc)
    row_own, *row_sends = row_hop(row_keep, from_core(row_send))
    up, down = first_hop(up_in, down_in, g3, g5)
    up_in, down_in = arrive(up, down)
    up_in[1], down_in[1] = tie((up_in[1], down_in[1]), row_own)
    up, down = hops(hop_kernel, up_in, down_in, g2, g6)
    up_in, down_in = arrive(up, down)
    row_parts = [row_own] + [from_x(row_sends[k - 1], -k) for k in (1, 2, 3)]
    up_in[1], down_in[1] = tie((up_in[1], down_in[1]), *row_parts)
    up, down = hops(hop_kernel, up_in, down_in, g1, g7)
    up_in, down_in = arrive(up, down)
    col_parts = []
    for q in p:
        own, *sends = last_hop(g0[q], up_in[q], down_in[q])
        col_parts += [own] + [from_y(sends[k - 1], -k) for k in (2, 1, 3)]
    return final(*row_parts, *col_parts)


def solution(mesh):
    placed = (
        P(("row", "col"), None),
        P(("row", "col")),
        P(("row", "col"), None),
        P(("row", "col"), None),
        P(("row", "col"), None, None, None),
        P(("row", "col"), None),
        P(("row", "col"), None),
        P(("row", "col"), None),
    )
    return jax.shard_map(
        local, mesh=mesh, in_specs=placed, out_specs=P(("row", "col"), None), check_vma=False
    )
```
